256 devices in a mesh: band: 32 (over z, y_lo, core), pw: 8 (over y_hi, x).
Axes of the slice: x: 4, y: 4 (y_hi: 2, y_lo: 2; y = y_hi * 2 + y_lo), z: 8, core: 2. Of those that a mesh axis runs over, the one named last changes fastest.
Arguments:
- elements: bfloat16 [64, 4096, 256], P('band', 'pw'), may hold values from -8 to 8
- strength: bfloat16 [4096, 4096], P('pw', 'band'), may hold values from -6 to 6
- pole_freq: bfloat16 [4096, 4096], P('pw', 'band'), may hold values from 0.5 to 4
- energies: float32 [64], P('band'), may hold values from -2 to 2
- imag_freqs: float32 [2], replicated, may hold values from 0.25 to 2
Outputs:
- sigma: float32 [2, 256, 256], P(None, 'band', 'pw')
The draws below stay inside these ranges and needn't reach their ends.
All inputs are finite; a program needn't handle non-finite values.
Results may differ from the reference program's by a relative error of at most 0.006.
Values may be sent and summed in bfloat16 or wider, within the bound.
A program may use at most 64 MiB of HBM per device.

```python
import math
import jax
import jax.numpy as jnp
from jax import lax

NS = 256
BAND_DEV = 2
NG = 4096
HB = 256
NBANDS = 64


def draw_elements(key, part):
    first, second = jax.random.split(jax.random.fold_in(key, 11), 2)
    shape = (NBANDS, NG, NS)
    base = jax.random.normal(first, shape, jnp.float32)
    groups = NBANDS // BAND_DEV
    pairing = jax.random.permutation(second, groups)
    band_group = jnp.arange(NBANDS) // BAND_DEV
    state_group = jnp.arange(NS) // (NS // groups)
    hit = pairing[band_group][:, None] == state_group[None, :]
    factor = jnp.where(hit, 2.5, 1.0)[:, None, :]
    return jnp.clip(base * factor, -8.0, 8.0).astype(jnp.bfloat16)


def draw_strength(key, part):
    first = jax.random.fold_in(jax.random.fold_in(key, 23), 0)
    shape = (NG, NG)
    base = jax.random.normal(first, shape, jnp.float32)
    return jnp.clip(base, -6.0, 6.0).astype(jnp.bfloat16)


def block_scale(stream_key, dims, cuts, least, largest):
    def one(dim, shards_of):
        heights = jax.random.uniform(jax.random.fold_in(jax.random.fold_in(stream_key, 6), dim), (shards_of,), jnp.float32, least / len(cuts), largest / len(cuts))
        return jnp.repeat(jnp.exp(heights), dims[dim] // shards_of).reshape((-1,) + (1,) * (len(dims) - dim - 1))

    gain = one(*cuts[0])
    for cut in cuts[1:]:
        gain = gain * one(*cut)
    return gain


def setup_inputs(seed: int = 0) -> dict:
    arg_keys = jax.random.split(jax.random.key(seed), 6)
    return {
        "elements": draw_elements(jax.random.fold_in(arg_keys[5], 71), 0),
        "strength": draw_strength(jax.random.fold_in(arg_keys[5], 71), 0),
        "pole_freq": jnp.clip(jnp.exp(math.log(4.0) - 2.0794415 * jax.random.uniform(arg_keys[2], (NG, NG), jnp.float32) ** block_scale(arg_keys[2], (NG, NG), ((0, 8), (1, 32)), -0.2, 0.2)), 0.5, 4.0).astype(jnp.bfloat16),
        "energies": jnp.clip(jax.random.uniform(arg_keys[3], (NBANDS,), jnp.float32, -2.0, 2.0) * block_scale(arg_keys[3], (NBANDS,), ((0, 32),), -0.4, 0.0), -2.0, 2.0),
        "imag_freqs": jnp.clip(jnp.exp(jax.random.uniform(arg_keys[4], (2,), jnp.float32, math.log(0.25), math.log(2.0))), 0.25, 2.0),
    }


def reference(elements, strength, pole_freq, energies, imag_freqs):
    nu_square = imag_freqs * imag_freqs
    strength_f = strength.astype(jnp.float32)
    pole_f = pole_freq.astype(jnp.float32)

    def one_band(running, inputs):
        band_rows, energy = inputs
        shifted = pole_f + energy
        kernel = (strength_f[None] * shifted[None] / (nu_square[:, None, None] + shifted[None] * shifted[None])).astype(jnp.bfloat16)
        rows_f = band_rows.astype(jnp.float32).reshape(NG // HB, HB, NS)
        kern_f = kernel.astype(jnp.float32).reshape(2, NG // HB, HB, NG)
        partial_value = jnp.einsum('rgn,ergc->ernc', rows_f, kern_f, precision=lax.Precision.HIGHEST).astype(jnp.bfloat16)
        running = running + jnp.einsum('ernc,cm->enm', partial_value.astype(jnp.float32), band_rows.astype(jnp.float32), precision=lax.Precision.HIGHEST)
        return (running, None)
    start = jnp.zeros((2, NS, NS), jnp.float32)
    total = lax.scan(one_band, start, (elements, energies))[0]
    return total / (NG * math.sqrt(NBANDS))
```

```python
import math

import jax
import jax.numpy as jnp
from jax import lax
from jax.experimental import pallas as pl
from jax.experimental.pallas import tpu as pltpu
from jax.sharding import PartitionSpec as P

MESH = pl.DeviceIdType.MESH
XS, YS, ZS = 4, 4, 8
BF = jnp.bfloat16
F32 = jnp.float32


def body(scale, e_ref, s_ref, w_ref, en_ref, nu_ref, out_ref,
         sw, et, xt, en, kbuf, pbuf, tbuf, rc, acc, rz, fin, rp,
         swap_s, swap_r, z_s, z_r, p_s, p_r, y_s, y_r, x_s, x_r, en_s, en_r,
         c_s, c_r, rz_s, rz_r, rp_s, rp_r):
    band, pw = lax.axis_index("band"), lax.axis_index("pw")
    z, y_lo, core = lax.div(band, 4), lax.rem(lax.div(band, 2), 2), lax.rem(band, 2)
    y_hi, x = lax.div(pw, 4), lax.rem(pw, 4)
    y = y_hi * 2 + y_lo
    quarter = y_lo * 2 + y_hi

    def dev(xx, yy, zz, cc):
        return ((zz * 2 + lax.rem(yy, 2)) * 2 + cc, lax.div(yy, 2) * 4 + xx)

    def zd(k):
        return dev(x, y, lax.rem(z + k + ZS, ZS), core)

    def yd(k):
        return dev(x, lax.rem(y + k + YS, YS), z, core)

    def xd(k):
        return dev(lax.rem(x + k + XS, XS), y, z, core)

    peer = dev(x, y, z, 1 - core)
    swapper = dev(x, core * 2 + y_lo, z, y_hi)
    swaps = y_hi != core

    def sum_partner(i):
        k, flip = i // 2, i % 2
        return dev(x, y_hi * 2 + lax.rem(y_lo + flip, 2), lax.rem(z + k, ZS), core)

    def pw_partner(i):
        return (band, lax.rem(pw + i, 8))

    barrier = pltpu.get_barrier_semaphore()
    others = [sum_partner(i) for i in range(1, 16)] + [pw_partner(i) for i in range(1, 8)]
    others += [dev(x, lax.rem(y + 3 + 2 * y_lo, YS), z, core), peer]
    for d in others:
        pl.semaphore_signal(barrier, inc=1, device_id=d, device_id_type=MESH)

    @pl.when(swaps)
    def _():
        pl.semaphore_signal(barrier, inc=1, device_id=swapper, device_id_type=MESH)

    for i in range(2):
        en[0, i] = jnp.full((8, 128), en_ref[i], F32)
    pl.semaphore_wait(barrier, len(others) + swaps.astype(jnp.int32))

    def copy(src, dst, ss, rs, d):
        return pltpu.make_async_remote_copy(
            src_ref=src, dst_ref=dst, send_sem=ss, recv_sem=rs, device_id=d, device_id_type=MESH)

    started = []

    def go(c):
        c.start()
        started.append(c)
        return c

    swap_copies = [copy(r, sw.at[0, y_hi, i], swap_s.at[i], swap_r.at[i], swapper)
                   for i, r in enumerate((s_ref, w_ref))]

    zc = {}
    for k in (0, 1, 2):
        zc[k + 1] = copy(sw.at[k, core], sw.at[k + 1, core], z_s.at[k + 1], z_r.at[k + 1], zd(1))
    for k in (0, 7, 6):
        to = (k - 1) % 8
        zc[to] = copy(sw.at[k, core], sw.at[to, core], z_s.at[to], z_r.at[to], zd(-1))
    zc[4] = copy(sw.at[3, core, 0], sw.at[4, core, 0], z_s.at[4], z_r.at[4], zd(1))
    zc[8] = copy(sw.at[5, core, 1], sw.at[4, core, 1], z_s.at[0], z_r.at[0], zd(-1))
    pc = [copy(sw.at[k, core], sw.at[k, core], p_s.at[k], p_r.at[k], peer) for k in range(8)]

    @pl.when(swaps)
    def _():
        for c in swap_copies:
            c.start()

    @pl.when(jnp.logical_not(swaps))
    def _():
        sw[0, core, 0] = s_ref[...]
        sw[0, core, 1] = w_ref[...]
        zc[1].start()
        zc[7].start()
        pc[0].start()

    for q in range(4):
        for b in range(2):
            et[0, q, b] = e_ref[b, q * 128:(q + 1) * 128, :].T

    yc = {
        1: copy(et.at[0], et.at[1], y_s.at[0], y_r.at[0], yd(1)),
        3: copy(et.at[0], et.at[3], y_s.at[1], y_r.at[1], yd(-1)),
        2: copy(et.at[1, pl.ds(0, 2)], et.at[2, pl.ds(0, 2)], y_s.at[2], y_r.at[2], yd(1)),
        4: copy(et.at[3, pl.ds(2, 2)], et.at[2, pl.ds(2, 2)], y_s.at[3], y_r.at[3], yd(-1)),
    }
    enc = copy(en.at[0], en.at[1], en_s, en_r, yd(1))
    xc = {}
    for j in range(4):
        xc[1, j] = copy(et.at[j, quarter], xt.at[1, j], x_s.at[j], x_r.at[j], xd(1))
        xc[3, j] = copy(et.at[j, quarter], xt.at[3, j], x_s.at[4 + j], x_r.at[4 + j], xd(-1))
        if j < 2:
            xc[2, j] = copy(xt.at[1, j], xt.at[2, j], x_s.at[8 + j], x_r.at[8 + j], xd(1))
        else:
            xc[2, j] = copy(xt.at[3, j], xt.at[2, j], x_s.at[8 + j], x_r.at[8 + j], xd(-1))

    go(yc[1])
    go(yc[3])
    go(enc)
    go(xc[1, 0])
    go(xc[3, 0])
    xt[0, 0] = et[0, quarter]

    @pl.when(swaps)
    def _():
        for c in swap_copies:
            c.wait()
        zc[1].start()
        zc[7].start()
        pc[0].start()

    started.extend([zc[1], zc[7], pc[0]])

    nu2 = [nu_ref[e] * nu_ref[e] for e in range(2)]

    def unit(t, p):
        k1 = t
        k2 = 8 - t - 4 * (1 - (t + 3) // 4)
        for bi in range(2):
            eps = en[p, bi, 0:1, :]
            eps = jnp.concatenate([eps, eps], axis=1)
            lhs = []
            for jj in range(2):
                j = p + 2 * jj
                r = lax.div(lax.rem(y - j + YS, YS), 2)
                for h in range(2):
                    rows = pl.ds(h * 256, 256)
                    s = jnp.concatenate([sw[k1, r, 0, rows, :], sw[k2, r, 0, rows, :]], axis=1).astype(F32)
                    w = jnp.concatenate([sw[k1, r, 1, rows, :], sw[k2, r, 1, rows, :]], axis=1).astype(F32)
                    v = w + eps
                    num = s * v
                    sq = v * v
                    for e in range(2):
                        kern = num * pl.reciprocal(sq + nu2[e], approx=True)
                        kbuf[bi, e, pl.ds(jj * 512 + h * 256, 256), :] = kern.astype(BF)
                for q in range(4):
                    lhs.append(et[j, q, bi])
            lhs = jnp.concatenate(lhs, axis=1)
            for e in range(2):
                part = jnp.dot(lhs, kbuf[bi, e], preferred_element_type=F32)
                pbuf[p * 4 + t, bi, e] = part.astype(BF)

    def second(i):
        p, t = lax.div(i, 4), lax.rem(i, 4)
        k1 = t
        k2 = 8 - t - 4 * (1 - (t + 3) // 4)
        group = lax.rem(y_lo + p, 2)

        def place(k):
            zz = lax.rem(z - k + ZS, ZS)
            j = lax.rem(y - (lax.div(zz, 4) * 2 + group) + YS, YS)
            return lax.rem(x - lax.rem(zz, 4) + XS, XS), j

        (i1, j1), (i2, j2) = place(k1), place(k2)
        for e in range(2):
            total = tbuf[e]
            for bi in range(2):
                right = jnp.concatenate([xt[i1, j1, bi], xt[i2, j2, bi]], axis=1)
                total = total + lax.dot_general(
                    pbuf[p * 4 + t, bi, e], right, (((1,), (1,)), ((), ())), preferred_element_type=F32)
            tbuf[e] = total

    def arrived_z(keys):
        for k in keys:
            zc[k].wait_recv()

    arrived_z((1, 7))
    go(zc[2])
    go(zc[6])
    go(pc[1])
    go(pc[7])
    xc[1, 0].wait_recv()
    xc[3, 0].wait_recv()
    go(xc[2, 0])
    arrived_z((2, 6))
    go(zc[3])
    go(zc[5])
    go(pc[2])
    go(pc[6])
    yc[1].wait_recv()
    yc[3].wait_recv()
    go(yc[2])
    go(yc[4])
    for j in (1, 3):
        go(xc[1, j])
        go(xc[3, j])
        xt[0, j] = et[j, quarter]
    enc.wait_recv()
    for k in (1, 7, 2, 6):
        pc[k].wait_recv()

    def first_loop(lo, hi, p):
        def step(t, c):
            unit(t, p)
            return c
        lax.fori_loop(lo, hi, step, 0)

    first_loop(1, 3, 1)
    for j in (1, 3):
        xc[1, j].wait_recv()
        xc[3, j].wait_recv()
    go(xc[2, 1])
    go(xc[2, 3])
    arrived_z((3, 5))
    go(zc[4])
    go(zc[8])
    go(pc[3])
    go(pc[5])
    yc[2].wait_recv()
    yc[4].wait_recv()
    go(xc[1, 2])
    go(xc[3, 2])
    xt[0, 2] = et[2, quarter]
    for k in (3, 5):
        pc[k].wait_recv()

    def mid(i, c):
        over = lax.div(i, 4)
        unit(i - over, over)
        return c

    lax.fori_loop(1, 3, mid, 0)
    arrived_z((4, 8))
    go(pc[4])
    xc[1, 2].wait_recv()
    xc[3, 2].wait_recv()
    go(xc[2, 2])
    lax.fori_loop(3, 5, mid, 0)
    pc[0].wait_recv()
    pc[4].wait_recv()

    def last(p, c):
        unit(0, p)
        return c

    lax.fori_loop(0, 2, last, 0)
    for j in range(4):
        xc[2, j].wait_recv()
    tbuf[...] = jnp.zeros_like(tbuf)

    def second_step(i, c):
        second(i)
        return c

    lax.fori_loop(0, 8, second_step, 0)

    for e in range(2):
        for i in range(16):
            for c in range(2):
                acc[c, i, e] = tbuf[e, (i * 2 + c) * 8:(i * 2 + c + 1) * 8, :] * scale
    cc = go(copy(acc.at[1 - core], rc, c_s, c_r, peer))
    cc.wait_recv()
    rc[...] = rc[...] + acc[core]
    mine = z * 2 + y_lo
    rz_copies = []
    for i in range(1, 16):
        k, flip = i // 2, i % 2
        to = lax.rem(z + k, ZS) * 2 + lax.rem(y_lo + flip, 2)
        rz_copies.append(go(copy(rc.at[to], rz.at[i], rz_s.at[i], rz_r.at[i], sum_partner(i))))
    total = rc[mine]
    for c in rz_copies:
        c.wait_recv()
    for i in range(1, 16):
        total = total + rz[i]
    fin[...] = total
    rp_copies = [go(copy(fin, rp.at[i], rp_s.at[i], rp_r.at[i], pw_partner(i))) for i in range(1, 8)]
    for c in rp_copies:
        c.wait_recv()
    for i in range(1, 8):
        total = total + rp[i]
    out_ref[...] = total
    for c in started:
        c.wait_send()


def on_device(elements, strength, pole_freq, energies, imag_freqs):
    states = elements.shape[2]
    scale = 1.0 / (4096 * math.sqrt(64))
    vm = pl.BlockSpec(memory_space=pltpu.VMEM)
    sm = pl.BlockSpec(memory_space=pltpu.SMEM)
    dma = pltpu.SemaphoreType.DMA
    out = pl.pallas_call(
        lambda *refs: body(scale, *refs),
        out_shape=jax.ShapeDtypeStruct((2, 8, states), F32),
        in_specs=[vm, vm, vm, sm, sm],
        out_specs=vm,
        scratch_shapes=[
            pltpu.VMEM((8, 2, 2, 512, 128), BF),
            pltpu.VMEM((4, 4, 2, 256, 128), BF),
            pltpu.VMEM((4, 4, 2, 256, 128), BF),
            pltpu.VMEM((2, 2, 8, 128), F32),
            pltpu.VMEM((2, 2, 1024, 256), BF),
            pltpu.VMEM((8, 2, 2, 256, 256), BF),
            pltpu.VMEM((2, 256, 256), F32),
            pltpu.VMEM((16, 2, 8, 256), F32),
            pltpu.VMEM((2, 16, 2, 8, 256), F32),
            pltpu.VMEM((16, 2, 8, 256), F32),
            pltpu.VMEM((2, 8, 256), F32),
            pltpu.VMEM((8, 2, 8, 256), F32),
            dma((2,)), dma((2,)),
            dma((8,)), dma((8,)),
            dma((8,)), dma((8,)),
            dma((4,)), dma((4,)),
            dma((12,)), dma((12,)),
            dma, dma,
            dma, dma,
            dma((16,)), dma((16,)),
            dma((8,)), dma((8,)),
        ],
        compiler_params=pltpu.CompilerParams(
            collective_id=0, has_side_effects=True, vmem_limit_bytes=40 * 1024 * 1024),
        cost_estimate=pl.CostEstimate(flops=6_500_000_000, bytes_accessed=1_000_000, transcendentals=8_000_000),
        name="self_energy",
    )(elements, strength, pole_freq, energies, imag_freqs)
    return lax.dynamic_slice_in_dim(out, lax.axis_index("pw") * 32, 32, 2)


def solution(mesh):
    in_specs = (P("band", "pw", None), P("pw", "band"), P("pw", "band"), P("band"), P())
    out_specs = P(None, "band", "pw")
    return jax.shard_map(
        on_device, mesh=mesh, in_specs=in_specs, out_specs=out_specs, check_vma=False
    )
```

```python
import math

import jax
import jax.numpy as jnp
from jax import lax
from jax.experimental import pallas as pl
from jax.experimental.pallas import tpu as pltpu
from jax.sharding import PartitionSpec as P

MESH = pl.DeviceIdType.MESH
XS, YS, ZS = 4, 4, 8
BF = jnp.bfloat16
F32 = jnp.float32


def body(scale, e_hbm, s_hbm, w_hbm, en_hbm, nu_hbm, out_ref,
         e_vm, en_sm, nu_sm, sw, et, xt, en, kbuf, pbuf, tbuf, rc, acc, sb, rz, fin, rp,
         in_s, swap_s, swap_r, z_s, z_r, p_s, p_r, y_s, y_r, x_s, x_r, en_s, en_r,
         c_s, c_r, rz_s, rz_r, rp_s, rp_r):
    band, pw = lax.axis_index("band"), lax.axis_index("pw")
    z, y_lo, core = lax.div(band, 4), lax.rem(lax.div(band, 2), 2), lax.rem(band, 2)
    y_hi, x = lax.div(pw, 4), lax.rem(pw, 4)
    y = y_hi * 2 + y_lo

    def quarter_of(k):
        yy = lax.rem(y + k + YS, YS)
        return lax.rem(yy, 2) * 2 + lax.div(yy, 2)

    quarter = quarter_of(0)

    def dev(xx, yy, zz, cc):
        return ((zz * 2 + lax.rem(yy, 2)) * 2 + cc, lax.div(yy, 2) * 4 + xx)

    def zd(k):
        return dev(x, y, lax.rem(z + k + ZS, ZS), core)

    def yd(k):
        return dev(x, lax.rem(y + k + YS, YS), z, core)

    def xd(k):
        return dev(lax.rem(x + k + XS, XS), y, z, core)

    peer = dev(x, y, z, 1 - core)
    swapper = dev(x, core * 2 + y_lo, z, y_hi)
    swaps = y_hi != core
    stays = jnp.logical_not(swaps)

    def sum_partner(i):
        k, flip = i // 2, i % 2
        return dev(x, y_hi * 2 + lax.rem(y_lo + flip, 2), lax.rem(z + k, ZS), core)

    def pw_partner(i):
        return (band, lax.rem(pw + i, 8))

    barrier = pltpu.get_barrier_semaphore()
    others = [sum_partner(i) for i in range(1, 16)] + [pw_partner(i) for i in range(1, 8)]
    others += [dev(x, lax.rem(y + 3 + 2 * y_lo, YS), z, core), peer]
    for d in others:
        pl.semaphore_signal(barrier, inc=1, device_id=d, device_id_type=MESH)

    @pl.when(swaps)
    def _():
        pl.semaphore_signal(barrier, inc=1, device_id=swapper, device_id_type=MESH)

    loads = [pltpu.make_async_copy(e_hbm.at[b], e_vm.at[b], in_s.at[b]) for b in range(2)]
    loads.append(pltpu.make_async_copy(en_hbm, en_sm, in_s.at[2]))
    loads.append(pltpu.make_async_copy(nu_hbm, nu_sm, in_s.at[3]))
    own_loads = [pltpu.make_async_copy(r, sw.at[0, core, i], in_s.at[4 + i]) for i, r in enumerate((s_hbm, w_hbm))]
    for c in loads:
        c.start()

    @pl.when(stays)
    def _():
        for c in own_loads:
            c.start()

    for c in loads:
        c.wait()
    for i in range(2):
        en[0, i] = jnp.full((8, 128), en_sm[i], F32)
    nu2 = [nu_sm[e] * nu_sm[e] for e in range(2)]
    for q in range(4):
        for b in range(2):
            et[0, q, b] = e_vm[b, q * 128:(q + 1) * 128, :].T

    def copy(src, dst, ss, rs, d):
        return pltpu.make_async_remote_copy(
            src_ref=src, dst_ref=dst, send_sem=ss, recv_sem=rs, device_id=d, device_id_type=MESH)

    started = []

    def go(*copies):
        for c in copies:
            c.start()
            started.append(c)

    swap_copies = [copy(r, sw.at[0, y_hi, i], swap_s.at[i], swap_r.at[i], swapper)
                   for i, r in enumerate((s_hbm, w_hbm))]

    zc = {}
    for i in range(2):
        for k in (1, 2, 3) + ((4,) if i == 0 else ()):
            zc[k, i] = copy(sw.at[k - 1, core, i], sw.at[k, core, i], z_s.at[k, i], z_r.at[k, i], zd(1))
        for k in (7, 6, 5) + ((4,) if i == 1 else ()):
            zc[k, i] = copy(sw.at[(k + 1) % 8, core, i], sw.at[k, core, i], z_s.at[k, i], z_r.at[k, i], zd(-1))
    pc = [copy(sw.at[k, core], sw.at[k, core], p_s.at[k], p_r.at[k], peer) for k in range(8)]

    yp, ym = {}, {}
    for a in range(4):
        q = quarter_of(a)
        yp[a] = copy(et.at[0, q], et.at[1, q], y_s.at[0, a], y_r.at[0, a], yd(1))
        ym[a] = copy(et.at[0, q], et.at[3, q], y_s.at[1, a], y_r.at[1, a], yd(-1))
    for a in (2, 0):
        q = quarter_of(a - 1)
        yp[4 + a] = copy(et.at[1, q], et.at[2, q], y_s.at[2, a], y_r.at[2, a], yd(1))
    for a in (3, 1):
        q = quarter_of(a + 1)
        ym[4 + a] = copy(et.at[3, q], et.at[2, q], y_s.at[2, a], y_r.at[2, a], yd(-1))
    enc = copy(en.at[0], en.at[1], en_s, en_r, yd(1))
    xp, xm, xr = {}, {}, {}
    for j in range(4):
        xp[j] = copy(et.at[j, quarter], xt.at[1, j], x_s.at[0, j], x_r.at[0, j], xd(1))
        xm[j] = copy(et.at[j, quarter], xt.at[3, j], x_s.at[1, j], x_r.at[1, j], xd(-1))
        xr[j] = (copy(xt.at[1, j, 0], xt.at[2, j, 0], x_s.at[2, j], x_r.at[2, j], xd(1)),
                 copy(xt.at[3, j, 1], xt.at[2, j, 1], x_s.at[3, j], x_r.at[3, j], xd(-1)))

    def kgen(k):
        t, side = (k, 0) if 0 <= k < 4 else ((8 - k) % 4, 1)

        def chunk(i, c):
            rows = pl.ds(pl.multiple_of(lax.rem(i, 8) * 64, 64), 64)
            s = sw[k, lax.div(i, 8), 0, rows, :].astype(F32)
            w = sw[k, lax.div(i, 8), 1, rows, :].astype(F32)
            to = pl.ds(pl.multiple_of(i * 64, 64), 64)
            for p in range(2):
                for bi in range(2):
                    v = w + en[p, bi, 0:1, :]
                    num = s * v
                    sq = v * v
                    for e in range(2):
                        kern = num * pl.reciprocal(sq + nu2[e], approx=True)
                        kbuf[t, side, p, bi, e, to, :] = kern.astype(BF)
            return c

        lax.fori_loop(0, 16, chunk, 0)

    def first(t, p):
        for bi in range(2):
            lhs = []
            for r in range(2):
                j = lax.rem(y - (r * 2 + lax.rem(y_lo + p, 2)) + YS, YS)
                for q in range(4):
                    lhs.append(et[j, q, bi])
            lhs = jnp.concatenate(lhs, axis=1)
            for e in range(2):
                right = jnp.concatenate([kbuf[t, 0, p, bi, e], kbuf[t, 1, p, bi, e]], axis=1)
                part = jnp.dot(lhs, right, preferred_element_type=F32)
                pbuf[p * 4 + t, bi, e] = part.astype(BF)

    def second(t, p):
        k1 = t
        k2 = 8 - t - 4 * (1 - (t + 3) // 4)
        group = lax.rem(y_lo + p, 2)

        def place(k):
            zz = lax.rem(z - k + ZS, ZS)
            j = lax.rem(y - (lax.div(zz, 4) * 2 + group) + YS, YS)
            return lax.rem(x - lax.rem(zz, 4) + XS, XS), j

        (i1, j1), (i2, j2) = place(k1), place(k2)
        for e in range(2):
            total = tbuf[e]
            for bi in range(2):
                right = jnp.concatenate([xt[i1, j1, bi], xt[i2, j2, bi]], axis=1)
                total = total + lax.dot_general(
                    pbuf[p * 4 + t, bi, e], right, (((1,), (1,)), ((), ())), preferred_element_type=F32)
            tbuf[e] = total

    def loop(f, p, lo, hi):
        def step(t, c):
            f(t, p)
            return c
        lax.fori_loop(lo, hi, step, 0)

    def z_pass(d):
        ks = (d, 8 - d)
        for i in range(2):
            for k in ks:
                zc[k, i].wait_recv()
                to = k + 1 if k == d else k - 1
                if (to, i) in zc and (to != 4 or i == (0 if k == d else 1)):
                    zc[to, i].start()
        for k in ks:
            pc[k].start()

    def own_start(i):
        zc[1, i].start()
        zc[7, i].start()

    pl.semaphore_wait(barrier, len(others) + swaps.astype(jnp.int32))

    @pl.when(swaps)
    def _():
        for c in swap_copies:
            c.start()

    @pl.when(stays)
    def _():
        for i in range(2):
            own_loads[i].wait()
            own_start(i)
        pc[0].start()

    go(enc, yp[2], ym[3], xp[0], xm[0], yp[1], ym[1])
    xt[0, 0] = et[0, quarter]
    tbuf[...] = jnp.zeros_like(tbuf)

    @pl.when(swaps)
    def _():
        for i in range(2):
            swap_copies[i].wait_recv()
            own_start(i)
        pc[0].start()

    @pl.when(stays)
    def _():
        z_pass(1)

    xp[0].wait_recv()
    xm[0].wait_recv()
    go(*xr[0])
    yp[2].wait_recv()
    go(yp[6], yp[0])
    ym[3].wait_recv()
    go(xp[3], xm[3])
    go(ym[7], ym[0])
    enc.wait_recv()

    @pl.when(stays)
    def _():
        z_pass(2)

    @pl.when(swaps)
    def _():
        z_pass(1)

    yp[1].wait_recv()
    go(xp[1], xm[1])
    ym[1].wait_recv()
    go(ym[5], yp[3], ym[2])
    xt[0, 1] = et[1, quarter]
    xt[0, 3] = et[3, quarter]
    pc[0].wait_recv()
    kgen(0)

    yp[6].wait_recv()
    go(xp[2], xm[2])
    xt[0, 2] = et[2, quarter]
    yp[0].wait_recv()
    go(yp[4])

    @pl.when(stays)
    def _():
        z_pass(3)

    @pl.when(swaps)
    def _():
        z_pass(2)

    for j in (3, 1):
        xp[j].wait_recv()
        xm[j].wait_recv()
        go(*xr[j])
    for k in (1, 7):
        pc[k].wait_recv()
        kgen(k)
    yp[3].wait_recv()
    for a in (0, 2):
        ym[a].wait_recv()
    xp[2].wait_recv()
    xm[2].wait_recv()
    go(*xr[2])

    @pl.when(swaps)
    def _():
        z_pass(3)

    loop(first, 1, 1, 2)
    for k in (2, 6):
        pc[k].wait_recv()
        kgen(k)

    @pl.when(stays)
    def _():
        zc[4, 0].wait_recv()
        zc[4, 1].wait_recv()
        pc[4].start()

    loop(first, 1, 2, 3)
    for k in (3, 5):
        pc[k].wait_recv()
        kgen(k)
    yp[4].wait_recv()
    ym[5].wait_recv()
    ym[7].wait_recv()
    loop(first, 0, 1, 4)

    @pl.when(swaps)
    def _():
        zc[4, 0].wait_recv()
        zc[4, 1].wait_recv()
        pc[4].start()

    loop(first, 1, 3, 4)
    for j in range(4):
        for c in xr[j]:
            c.wait_recv()
    loop(second, 0, 1, 4)
    loop(second, 1, 1, 4)
    pc[4].wait_recv()
    kgen(4)
    for p in range(2):
        first(0, p)
        second(0, p)

    for e in range(2):
        for i in range(16):
            for c in range(2):
                acc[c, i, e * 8:(e + 1) * 8, :] = tbuf[e, (i * 2 + c) * 8:(i * 2 + c + 1) * 8, :] * scale
    cc = copy(acc.at[1 - core], rc, c_s, c_r, peer)
    go(cc)
    cc.wait_recv()
    for i in range(16):
        sb[i] = (rc[i] + acc[core, i]).astype(BF)
    mine = z * 2 + y_lo
    rz_copies = []
    for i in range(1, 16):
        k, flip = i // 2, i % 2
        to = lax.rem(z + k, ZS) * 2 + lax.rem(y_lo + flip, 2)
        rz_copies.append(copy(sb.at[to], rz.at[i], rz_s.at[i], rz_r.at[i], sum_partner(i)))
    go(*rz_copies)
    total = rc[mine] + acc[core, mine]
    for c in rz_copies:
        c.wait_recv()
    for i in range(1, 16):
        total = total + rz[i].astype(F32)
    fin[...] = total
    rp_copies = [copy(fin, rp.at[i], rp_s.at[i], rp_r.at[i], pw_partner(i)) for i in range(1, 8)]
    go(*rp_copies)
    for c in rp_copies:
        c.wait_recv()
    for i in range(1, 8):
        total = total + rp[i]
    for e in range(2):
        out_ref[e] = total[e * 8:(e + 1) * 8, :]
    for c in started:
        c.wait_send()
    for c in list(zc.values()) + pc:
        c.wait_send()

    @pl.when(swaps)
    def _():
        for c in swap_copies:
            c.wait_send()


def on_device(elements, strength, pole_freq, energies, imag_freqs):
    states = elements.shape[2]
    scale = 1.0 / (4096 * math.sqrt(64))
    vm = pl.BlockSpec(memory_space=pltpu.VMEM)
    hbm = pl.BlockSpec(memory_space=pltpu.HBM)
    dma = pltpu.SemaphoreType.DMA
    out = pl.pallas_call(
        lambda *refs: body(scale, *refs),
        out_shape=jax.ShapeDtypeStruct((2, 8, states), F32),
        in_specs=[hbm] * 5,
        out_specs=vm,
        scratch_shapes=[
            pltpu.VMEM((2, 512, 256), BF),
            pltpu.SMEM((2,), F32),
            pltpu.SMEM((2,), F32),
            pltpu.VMEM((8, 2, 2, 512, 128), BF),
            pltpu.VMEM((4, 4, 2, 256, 128), BF),
            pltpu.VMEM((4, 4, 2, 256, 128), BF),
            pltpu.VMEM((2, 2, 8, 128), F32),
            pltpu.VMEM((4, 2, 2, 2, 2, 1024, 128), BF),
            pltpu.VMEM((8, 2, 2, 256, 256), BF),
            pltpu.VMEM((2, 256, 256), F32),
            pltpu.VMEM((16, 16, 256), F32),
            pltpu.VMEM((2, 16, 16, 256), F32),
            pltpu.VMEM((16, 16, 256), BF),
            pltpu.VMEM((16, 16, 256), BF),
            pltpu.VMEM((16, 256), F32),
            pltpu.VMEM((8, 16, 256), F32),
            dma((6,)),
            dma((2,)), dma((2,)),
            dma((8, 2)), dma((8, 2)),
            dma((8,)), dma((8,)),
            dma((3, 4)), dma((3, 4)),
            dma((4, 4)), dma((4, 4)),
            dma, dma,
            dma, dma,
            dma((16,)), dma((16,)),
            dma((8,)), dma((8,)),
        ],
        compiler_params=pltpu.CompilerParams(
            collective_id=0, has_side_effects=True, vmem_limit_bytes=63 * 1024 * 1024),
        cost_estimate=pl.CostEstimate(flops=6_500_000_000, bytes_accessed=1_000_000, transcendentals=8_000_000),
        name="self_energy",
    )(elements, strength, pole_freq, energies, imag_freqs)
    return lax.dynamic_slice_in_dim(out, lax.axis_index("pw") * 32, 32, 2)


def solution(mesh):
    in_specs = (P("band", "pw", None), P("pw", "band"), P("pw", "band"), P("band"), P())
    out_specs = P(None, "band", "pw")
    return jax.shard_map(
        on_device, mesh=mesh, in_specs=in_specs, out_specs=out_specs, check_vma=False
    )
```

```python
import math

import jax
import jax.numpy as jnp
from jax import lax
from jax.experimental import pallas as pl
from jax.experimental.pallas import tpu as pltpu
from jax.sharding import PartitionSpec as P

MESH = pl.DeviceIdType.MESH
XS, YS, ZS = 4, 4, 8
BF = jnp.bfloat16
F32 = jnp.float32


def body(scale, e_hbm, s_hbm, w_hbm, en_hbm, nu_hbm, out_ref,
         e_vm, en_sm, nu_sm, sw, et, xt, en, kbuf, pacc, pbuf, tbuf, rc, acc, sb, rz, fin, rp,
         in_s, swap_s, swap_r, z_s, z_r, p_s, p_r, y_s, y_r, x_s, x_r, en_s, en_r,
         c_s, c_r, rz_s, rz_r, rp_s, rp_r, tok):
    band, pw = lax.axis_index("band"), lax.axis_index("pw")
    z, y_lo, core = lax.div(band, 4), lax.rem(lax.div(band, 2), 2), lax.rem(band, 2)
    y_hi, x = lax.div(pw, 4), lax.rem(pw, 4)
    y = y_hi * 2 + y_lo

    def quarter_of(k):
        yy = lax.rem(y + k + YS, YS)
        return lax.rem(yy, 2) * 2 + lax.div(yy, 2)

    quarter = quarter_of(0)

    def dev(xx, yy, zz, cc):
        return ((zz * 2 + lax.rem(yy, 2)) * 2 + cc, lax.div(yy, 2) * 4 + xx)

    def zd(k):
        return dev(x, y, lax.rem(z + k + ZS, ZS), core)

    def yd(k):
        return dev(x, lax.rem(y + k + YS, YS), z, core)

    def xd(k):
        return dev(lax.rem(x + k + XS, XS), y, z, core)

    peer = dev(x, y, z, 1 - core)
    swapper = dev(x, core * 2 + y_lo, z, y_hi)
    swaps = y_hi != core
    stays = jnp.logical_not(swaps)

    def sum_partner(i):
        k, flip = i // 2, i % 2
        return dev(x, y_hi * 2 + lax.rem(y_lo + flip, 2), lax.rem(z + k, ZS), core)

    def pw_partner(i):
        return (band, lax.rem(pw + i, 8))

    barrier = pltpu.get_barrier_semaphore()
    others = [zd(1), zd(-1), yd(1), yd(-1), xd(1), xd(-1), peer]
    for d in others:
        pl.semaphore_signal(barrier, inc=1, device_id=d, device_id_type=MESH)

    @pl.when(swaps)
    def _():
        pl.semaphore_signal(barrier, inc=1, device_id=swapper, device_id_type=MESH)

    loads = [pltpu.make_async_copy(e_hbm.at[b], e_vm.at[b], in_s.at[b]) for b in range(2)]
    loads.append(pltpu.make_async_copy(en_hbm, en_sm, in_s.at[2]))
    loads.append(pltpu.make_async_copy(nu_hbm, nu_sm, in_s.at[3]))
    own_loads = [pltpu.make_async_copy(r, sw.at[0, core, i], in_s.at[4 + i]) for i, r in enumerate((s_hbm, w_hbm))]
    for c in loads:
        c.start()

    @pl.when(stays)
    def _():
        for c in own_loads:
            c.start()

    for c in loads:
        c.wait()
    for i in range(2):
        en[0, i] = jnp.full((8, 128), en_sm[i], F32)
    nu2 = [nu_sm[e] * nu_sm[e] for e in range(2)]
    for q in range(4):
        for b in range(2):
            et[0, q, b] = e_vm[b, q * 128:(q + 1) * 128, :].T

    def copy(src, dst, ss, rs, d):
        return pltpu.make_async_remote_copy(
            src_ref=src, dst_ref=dst, send_sem=ss, recv_sem=rs, device_id=d, device_id_type=MESH)

    started = []

    def go(*copies):
        for c in copies:
            c.start()
            if all(c is not o for o in started):
                started.append(c)

    chunks = [(i, pl.ds(h * 256, 256)) for i in range(2) for h in range(2)]
    own_refs = (s_hbm, w_hbm)
    swap_copies = [copy(own_refs[i].at[rows, :], sw.at[0, y_hi, i, rows, :], swap_s.at[n], swap_r.at[n], swapper)
                   for n, (i, rows) in enumerate(chunks)]

    zc = {}
    for n, (i, rows) in enumerate(chunks):
        for k in (1, 2, 3) + ((4,) if i == 0 else ()):
            zc[k, n] = copy(sw.at[k - 1, core, i, rows, :], sw.at[k, core, i, rows, :], z_s.at[k, n], z_r.at[k, n], zd(1))
        for k in (7, 6, 5) + ((4,) if i == 1 else ()):
            zc[k, n] = copy(sw.at[(k + 1) % 8, core, i, rows, :], sw.at[k, core, i, rows, :], z_s.at[k, n], z_r.at[k, n],
                            zd(-1))
    pc = [copy(sw.at[k, core], sw.at[k, core], p_s.at[k], p_r.at[k], peer) for k in range(8)]

    yp, ym = {}, {}
    for a in range(4):
        q = quarter_of(a)
        yp[a] = copy(et.at[0, q], et.at[1, q], y_s.at[0, a], y_r.at[0, a], yd(1))
        ym[a] = copy(et.at[0, q], et.at[3, q], y_s.at[1, a], y_r.at[1, a], yd(-1))
    for a in (2, 0):
        q = quarter_of(a - 1)
        yp[4 + a] = copy(et.at[1, q], et.at[2, q], y_s.at[2, a], y_r.at[2, a], yd(1))
    for a in (3, 1):
        q = quarter_of(a + 1)
        ym[4 + a] = copy(et.at[3, q], et.at[2, q], y_s.at[2, a], y_r.at[2, a], yd(-1))
    enc = copy(en.at[0], en.at[1], en_s, en_r, yd(1))
    xp, xm, xr = {}, {}, {}
    for j in range(4):
        xp[j] = copy(et.at[j, quarter], xt.at[1, j], x_s.at[0, j], x_r.at[0, j], xd(1))
        xm[j] = copy(et.at[j, quarter], xt.at[3, j], x_s.at[1, j], x_r.at[1, j], xd(-1))
        xr[j] = (copy(xt.at[1, j, 0], xt.at[2, j, 0], x_s.at[2, j], x_r.at[2, j], xd(1)),
                 copy(xt.at[3, j, 1], xt.at[2, j, 1], x_s.at[3, j], x_r.at[3, j], xd(-1)))

    def kgen(k, r):
        t, side = (k, 0) if 0 <= k < 4 else ((8 - k) % 4, 1)

        def chunk(i, c):
            rows = pl.ds(pl.multiple_of(i * 128, 128), 128)
            s = sw[k, r, 0, rows, :].astype(F32)
            w = sw[k, r, 1, rows, :].astype(F32)
            to = pl.ds(pl.multiple_of(r * 512 + i * 128, 128), 128)
            for p in range(2):
                for bi in range(2):
                    v = w + en[p, bi, 0:1, :]
                    num = s * v
                    sq = v * v
                    a0, a1 = sq + nu2[0], sq + nu2[1]
                    both = num * pl.reciprocal(a0 * a1, approx=True)
                    kbuf[t, side, p, bi, 0, to, :] = (both * a1).astype(BF)
                    kbuf[t, side, p, bi, 1, to, :] = (both * a0).astype(BF)
            return c

        lax.fori_loop(0, 4, chunk, 0)

    def pieces(p, part):
        if p == 0:
            return [(2 * part, quarter_of(a), lax.div(lax.rem(y + 2 * part, YS), 2)) for a in range(4)]
        below, above = lax.div(lax.rem(y + 3, YS), 2), lax.div(lax.rem(y + 1, YS), 2)
        if part == 0:
            return [(1, quarter_of(1), below), (1, quarter_of(0), below), (3, quarter_of(0), above), (3, quarter_of(2), above)]
        return [(1, quarter_of(3), below), (1, quarter_of(2), below), (3, quarter_of(1), above), (3, quarter_of(3), above)]

    def block_pieces(p, r):
        j = lax.rem(y - (r * 2 + lax.rem(y_lo + p, 2)) + YS, YS)
        return [(j, q, r) for q in range(4)]

    def product(t, p, some, bi, e):
        left = jnp.concatenate([et[j, q, bi] for j, q, r in some], axis=1)
        right = []
        for j, q, r in some:
            rows = pl.ds(pl.multiple_of(r * 512 + q * 128, 128), 128)
            right.append(jnp.concatenate([kbuf[t, side, p, bi, e, rows, :] for side in range(2)], axis=1))
        return jnp.dot(left, jnp.concatenate(right, axis=0), preferred_element_type=F32)

    def first(t, p, part, some):
        for bi in range(2):
            for e in range(2):
                value = product(t, p, some, bi, e)
                if part == 0:
                    pacc[p * 4 + t, bi, e] = value
                else:
                    pbuf[p * 4 + t, bi, e] = (pacc[p * 4 + t, bi, e] + value).astype(BF)

    def whole(p, lo, hi):
        def step(t, c):
            for bi in range(2):
                for e in range(2):
                    value = product(t, p, pieces(p, 0) + pieces(p, 1), bi, e)
                    pbuf[p * 4 + t, bi, e] = value.astype(BF)
            return c
        lax.fori_loop(lo, hi, step, 0)

    def place(k, p):
        zz = lax.rem(z - k + ZS, ZS)
        j = lax.rem(y - (lax.div(zz, 4) * 2 + lax.rem(y_lo + p, 2)) + YS, YS)
        return lax.rem(x - lax.rem(zz, 4) + XS, XS), j

    def second(ts, ps, fresh, es=(0, 1)):
        for e in es:
            left, right = [], []
            for p in ps:
                for t in ts:
                    (i1, j1), (i2, j2) = place(t, p), place((8 - t) if t else 4, p)
                    for bi in range(2):
                        left.append(pbuf[p * 4 + t, bi, e])
                        right.append(jnp.concatenate([xt[i1, j1, bi], xt[i2, j2, bi]], axis=1))
            value = lax.dot_general(
                jnp.concatenate(left, axis=1), jnp.concatenate(right, axis=1), (((1,), (1,)), ((), ())),
                preferred_element_type=F32)
            tbuf[e] = value if fresh else tbuf[e] + value

    def loop(p, part, lo, hi):
        def step(t, c):
            first(t, p, part, pieces(p, part))
            return c
        lax.fori_loop(lo, hi, step, 0)

    def z_pass(d, ns):
        for n in ns:
            for k, to in ((d, d + 1), (8 - d, 7 - d)):
                zc[k, n].wait_recv()
                if to != 4 or (n < 2) == (k == d):
                    zc[to, n].start()
        if 3 in ns:
            pc[d].start()
            pc[8 - d].start()
            if d > 1:
                token_wait(d - 2)
                token(d - 1)

    def last_tokens():
        token_wait(2)
        token(3, (0,))

    def z_end():
        for n in range(4):
            zc[4, n].wait_recv()
        pc[4].start()

    def own(*ks):
        for k in ks:
            kgen(k, core)

    def other(*ks):
        for k in ks:
            pc[k].wait_recv()
            kgen(k, 1 - core)

    def token(n, ways=(0, 1)):
        for w in ways:
            pl.semaphore_signal(tok.at[w, n], inc=1, device_id=zd(1 - 2 * w), device_id_type=MESH)

    def token_wait(n, ways=(0, 1)):
        for w in ways:
            pl.semaphore_wait(tok.at[w, n], 1)

    def x_on(j):
        xp[j].wait_recv()
        xm[j].wait_recv()
        go(*xr[j])

    def y_one():
        yp[2].wait_recv()
        go(yp[6], yp[0])
        ym[3].wait_recv()
        go(xp[3], xm[3])
        go(ym[7], ym[0])
        token(0)

    def y_two():
        yp[1].wait_recv()
        go(xp[1], xm[1])
        ym[1].wait_recv()
        go(ym[5], yp[3], ym[2])
        xt[0, 1] = et[1, quarter]
        xt[0, 3] = et[3, quarter]

    def y_three():
        yp[6].wait_recv()
        go(xp[2], xm[2])
        xt[0, 2] = et[2, quarter]

    def y_four():
        yp[0].wait_recv()
        go(yp[4])

    def y_five():
        yp[3].wait_recv()
        ym[0].wait_recv()
        ym[2].wait_recv()

    def y_six():
        for c in (yp[4], ym[5], ym[7]):
            c.wait_recv()

    def start():
        go(enc, yp[2], ym[3], xp[0], xm[0], yp[1], ym[1])
        xt[0, 0] = et[0, quarter]

    def finish():
        for j in range(4):
            for c in xr[j]:
                c.wait_recv()
        second((1, 2, 3), (0, 1), True)

    pl.semaphore_wait(barrier, len(others) + swaps.astype(jnp.int32))
    every = range(4)

    @pl.when(stays)
    def _():
        for i in range(2):
            own_loads[i].wait()
        for n in every:
            zc[1, n].start()
            zc[7, n].start()
        pc[0].start()
        start()
        enc.wait_recv()
        own(0)
        z_pass(1, every)
        x_on(0)
        own(1)
        z_pass(2, (0, 1))
        own(7)
        y_one()
        z_pass(2, (2, 3))
        other(0)
        own(2, 6)
        y_two()
        z_pass(3, (0, 1))
        other(1)
        z_pass(3, (2, 3))
        other(7)
        y_three()
        loop(0, 0, 1, 2)
        x_on(3)
        own(3, 5)
        y_four()
        loop(1, 0, 1, 2)
        other(2)
        x_on(1)
        z_end()
        last_tokens()
        other(6)
        loop(0, 0, 2, 3)
        own(4)
        loop(1, 0, 2, 3)
        y_five()
        x_on(2)
        other(3)
        loop(1, 1, 1, 3)
        other(5)
        loop(0, 0, 3, 4)
        whole(1, 3, 4)
        y_six()
        loop(0, 1, 1, 4)
        for p in range(2):
            first(0, p, 0, block_pieces(p, core))
        finish()
        other(4)
        for p in range(2):
            first(0, p, 1, block_pieces(p, 1 - core))

    @pl.when(swaps)
    def _():
        for c in swap_copies:
            c.start()
        start()
        for n in every:
            swap_copies[n].wait_recv()
            zc[1, n].start()
            zc[7, n].start()
        pc[0].start()
        enc.wait_recv()
        x_on(0)
        other(0)
        own(0)
        other(1)
        z_pass(1, (0,))
        y_one()
        z_pass(1, (1, 2, 3))
        own(1)
        y_two()
        own(7)
        other(7)
        z_pass(2, (0, 1))
        loop(0, 0, 1, 2)
        other(2)
        y_three()
        z_pass(2, (2, 3))
        loop(1, 0, 1, 2)
        other(6)
        x_on(3)
        own(2)
        z_pass(3, (0, 1))
        y_four()
        own(6)
        loop(0, 0, 2, 3)
        x_on(1)
        other(3)
        z_pass(3, (2, 3))
        own(3)
        y_five()
        x_on(2)
        last_tokens()
        other(5)
        own(5)
        loop(1, 1, 1, 2)
        loop(0, 0, 3, 4)
        whole(1, 2, 4)
        other(4)
        y_six()
        loop(0, 1, 1, 4)
        for p in range(2):
            first(0, p, 0, block_pieces(p, 1 - core))
        z_end()
        finish()
        own(4)
        for p in range(2):
            first(0, p, 1, block_pieces(p, core))

    core_copies = []
    for e in range(2):
        second((0,), (0, 1), False, (e,))
        for i in range(16):
            for c in range(2):
                acc[c, e, i] = tbuf[e, (i * 2 + c) * 8:(i * 2 + c + 1) * 8, :] * scale
        core_copies.append(copy(acc.at[1 - core, e], rc.at[e], c_s.at[e], c_r.at[e], peer))
        go(core_copies[e])
    token_wait(3, (0,))
    for e in range(2):
        core_copies[e].wait_recv()
    for i in range(16):
        both = jnp.concatenate([rc[e, i] + acc[core, e, i] for e in range(2)], axis=0)
        sb[i] = both.astype(BF)
    mine = z * 2 + y_lo
    rz_copies = []
    for i in range(1, 16):
        k, flip = i // 2, i % 2
        to = lax.rem(z + k, ZS) * 2 + lax.rem(y_lo + flip, 2)
        rz_copies.append(copy(sb.at[to], rz.at[i], rz_s.at[i], rz_r.at[i], sum_partner(i)))
    go(*rz_copies)
    total = jnp.concatenate([rc[e, mine] + acc[core, e, mine] for e in range(2)], axis=0)
    for c in rz_copies:
        c.wait_recv()
    for i in range(1, 16):
        total = total + rz[i].astype(F32)
    fin[...] = total
    rp_copies = [copy(fin, rp.at[i], rp_s.at[i], rp_r.at[i], pw_partner(i)) for i in range(1, 8)]
    go(*rp_copies)
    for c in rp_copies:
        c.wait_recv()
    for i in range(1, 8):
        total = total + rp[i]
    for e in range(2):
        out_ref[e] = total[e * 8:(e + 1) * 8, :]
    for c in started:
        c.wait_send()
    for c in list(zc.values()) + pc:
        c.wait_send()

    @pl.when(swaps)
    def _():
        for c in swap_copies:
            c.wait_send()


def on_device(elements, strength, pole_freq, energies, imag_freqs):
    states = elements.shape[2]
    scale = 1.0 / (4096 * math.sqrt(64))
    vm = pl.BlockSpec(memory_space=pltpu.VMEM)
    hbm = pl.BlockSpec(memory_space=pltpu.HBM)
    dma = pltpu.SemaphoreType.DMA
    out = pl.pallas_call(
        lambda *refs: body(scale, *refs),
        out_shape=jax.ShapeDtypeStruct((2, 8, states), F32),
        in_specs=[hbm] * 5,
        out_specs=vm,
        scratch_shapes=[
            pltpu.VMEM((2, 512, 256), BF),
            pltpu.SMEM((2,), F32),
            pltpu.SMEM((2,), F32),
            pltpu.VMEM((8, 2, 2, 512, 128), BF),
            pltpu.VMEM((4, 4, 2, 256, 128), BF),
            pltpu.VMEM((4, 4, 2, 256, 128), BF),
            pltpu.VMEM((2, 2, 8, 128), F32),
            pltpu.VMEM((4, 2, 2, 2, 2, 1024, 128), BF),
            pltpu.VMEM((8, 2, 2, 256, 256), F32),
            pltpu.VMEM((8, 2, 2, 256, 256), BF),
            pltpu.VMEM((2, 256, 256), F32),
            pltpu.VMEM((2, 16, 8, 256), F32),
            pltpu.VMEM((2, 2, 16, 8, 256), F32),
            pltpu.VMEM((16, 16, 256), BF),
            pltpu.VMEM((16, 16, 256), BF),
            pltpu.VMEM((16, 256), F32),
            pltpu.VMEM((8, 16, 256), F32),
            dma((6,)),
            dma((4,)), dma((4,)),
            dma((8, 4)), dma((8, 4)),
            dma((8,)), dma((8,)),
            dma((3, 4)), dma((3, 4)),
            dma((4, 4)), dma((4, 4)),
            dma, dma,
            dma((2,)), dma((2,)),
            dma((16,)), dma((16,)),
            dma((8,)), dma((8,)),
            pltpu.SemaphoreType.REGULAR((2, 4)),
        ],
        compiler_params=pltpu.CompilerParams(
            collective_id=0, has_side_effects=True, vmem_limit_bytes=63 * 1024 * 1024),
        cost_estimate=pl.CostEstimate(flops=6_500_000_000, bytes_accessed=1_000_000, transcendentals=8_000_000),
        name="self_energy",
    )(elements, strength, pole_freq, energies, imag_freqs)
    return lax.dynamic_slice_in_dim(out, lax.axis_index("pw") * 32, 32, 2)


def solution(mesh):
    in_specs = (P("band", "pw", None), P("pw", "band"), P("pw", "band"), P("band"), P())
    out_specs = P(None, "band", "pw")
    return jax.shard_map(
        on_device, mesh=mesh, in_specs=in_specs, out_specs=out_specs, check_vma=False
    )
```

```python
import math

import jax
import jax.numpy as jnp
from jax import lax
from jax.experimental import pallas as pl
from jax.experimental.pallas import tpu as pltpu
from jax.sharding import PartitionSpec as P

MESH = pl.DeviceIdType.MESH
XS, YS, ZS = 4, 4, 8
BF = jnp.bfloat16
F32 = jnp.float32


def body(scale, e_hbm, s_hbm, w_hbm, en_hbm, nu_hbm, out_ref,
         e_vm, en_sm, nu_sm, sw, et, xt, en, kbuf, pacc, pbuf, tbuf, rc, acc, sb, rz, fin, rp,
         in_s, swap_s, swap_r, z_s, z_r, p_s, p_r, y_s, y_r, x_s, x_r, en_s, en_r,
         c_s, c_r, rz_s, rz_r, rp_s, rp_r, tok):
    band, pw = lax.axis_index("band"), lax.axis_index("pw")
    z, y_lo, core = lax.div(band, 4), lax.rem(lax.div(band, 2), 2), lax.rem(band, 2)
    y_hi, x = lax.div(pw, 4), lax.rem(pw, 4)
    y = y_hi * 2 + y_lo

    def quarter_of(k):
        yy = lax.rem(y + k + YS, YS)
        return lax.rem(yy, 2) * 2 + lax.div(yy, 2)

    quarter = quarter_of(0)

    def dev(xx, yy, zz, cc):
        return ((zz * 2 + lax.rem(yy, 2)) * 2 + cc, lax.div(yy, 2) * 4 + xx)

    def zd(k):
        return dev(x, y, lax.rem(z + k + ZS, ZS), core)

    def yd(k):
        return dev(x, lax.rem(y + k + YS, YS), z, core)

    def xd(k):
        return dev(lax.rem(x + k + XS, XS), y, z, core)

    peer = dev(x, y, z, 1 - core)
    swapper = dev(x, core * 2 + y_lo, z, y_hi)
    swaps = y_hi != core
    stays = jnp.logical_not(swaps)

    def sum_partner(i):
        k, flip = i // 2, i % 2
        return dev(x, y_hi * 2 + lax.rem(y_lo + flip, 2), lax.rem(z + k, ZS), core)

    def pw_partner(i):
        return (band, lax.rem(pw + i, 8))

    barrier = pltpu.get_barrier_semaphore()
    others = [zd(1), zd(-1), yd(1), yd(-1), xd(1), xd(-1), peer]
    for d in others:
        pl.semaphore_signal(barrier, inc=1, device_id=d, device_id_type=MESH)

    @pl.when(swaps)
    def _():
        pl.semaphore_signal(barrier, inc=1, device_id=swapper, device_id_type=MESH)

    loads = [pltpu.make_async_copy(e_hbm.at[b], e_vm.at[b], in_s.at[b]) for b in range(2)]
    loads.append(pltpu.make_async_copy(en_hbm, en_sm, in_s.at[2]))
    loads.append(pltpu.make_async_copy(nu_hbm, nu_sm, in_s.at[3]))
    own_loads = [pltpu.make_async_copy(r, sw.at[0, core, i], in_s.at[4 + i]) for i, r in enumerate((s_hbm, w_hbm))]
    for c in loads:
        c.start()

    @pl.when(stays)
    def _():
        for c in own_loads:
            c.start()

    for c in loads:
        c.wait()
    for i in range(2):
        en[0, i] = jnp.full((8, 128), en_sm[i], F32)
    nu2 = [nu_sm[e] * nu_sm[e] for e in range(2)]
    for q in range(4):
        for b in range(2):
            et[0, q, b] = e_vm[b, q * 128:(q + 1) * 128, :].T

    def copy(src, dst, ss, rs, d):
        return pltpu.make_async_remote_copy(
            src_ref=src, dst_ref=dst, send_sem=ss, recv_sem=rs, device_id=d, device_id_type=MESH)

    started = []

    def go(*copies):
        for c in copies:
            c.start()
            if all(c is not o for o in started):
                started.append(c)

    chunks = [(i, pl.ds(h * 256, 256)) for i in range(2) for h in range(2)]
    own_refs = (s_hbm, w_hbm)
    swap_copies = [copy(own_refs[i].at[rows, :], sw.at[0, y_hi, i, rows, :], swap_s.at[n], swap_r.at[n], swapper)
                   for n, (i, rows) in enumerate(chunks)]

    zc = {}
    for n, (i, rows) in enumerate(chunks):
        for k in (1, 2, 3) + ((4,) if i == 0 else ()):
            zc[k, n] = copy(sw.at[k - 1, core, i, rows, :], sw.at[k, core, i, rows, :], z_s.at[k, n], z_r.at[k, n], zd(1))
        for k in (7, 6, 5) + ((4,) if i == 1 else ()):
            zc[k, n] = copy(sw.at[(k + 1) % 8, core, i, rows, :], sw.at[k, core, i, rows, :], z_s.at[k, n], z_r.at[k, n],
                            zd(-1))
    pc = [copy(sw.at[k, core], sw.at[k, core], p_s.at[k], p_r.at[k], peer) for k in range(8)]

    yp, ym = {}, {}
    for a in range(4):
        q = quarter_of(a)
        yp[a] = copy(et.at[0, q], et.at[1, q], y_s.at[0, a], y_r.at[0, a], yd(1))
        ym[a] = copy(et.at[0, q], et.at[3, q], y_s.at[1, a], y_r.at[1, a], yd(-1))
    for a in (2, 0):
        q = quarter_of(a - 1)
        yp[4 + a] = copy(et.at[1, q], et.at[2, q], y_s.at[2, a], y_r.at[2, a], yd(1))
    for a in (3, 1):
        q = quarter_of(a + 1)
        ym[4 + a] = copy(et.at[3, q], et.at[2, q], y_s.at[2, a], y_r.at[2, a], yd(-1))
    enc = copy(en.at[0], en.at[1], en_s, en_r, yd(1))
    xp, xm, xr = {}, {}, {}
    for j in range(4):
        xp[j] = copy(et.at[j, quarter], xt.at[1, j], x_s.at[0, j], x_r.at[0, j], xd(1))
        xm[j] = copy(et.at[j, quarter], xt.at[3, j], x_s.at[1, j], x_r.at[1, j], xd(-1))
        xr[j] = (copy(xt.at[1, j, 0], xt.at[2, j, 0], x_s.at[2, j], x_r.at[2, j], xd(1)),
                 copy(xt.at[3, j, 1], xt.at[2, j, 1], x_s.at[3, j], x_r.at[3, j], xd(-1)))

    def kgen(k, r):
        t, side = (k, 0) if 0 <= k < 4 else ((8 - k) % 4, 1)

        def chunk(i, c):
            rows = pl.ds(pl.multiple_of(i * 128, 128), 128)
            s = sw[k, r, 0, rows, :].astype(F32)
            w = sw[k, r, 1, rows, :].astype(F32)
            to = pl.ds(pl.multiple_of(r * 512 + i * 128, 128), 128)
            for p in range(2):
                for bi in range(2):
                    v = w + en[p, bi, 0:1, :]
                    num = s * v
                    sq = v * v
                    a0, a1 = sq + nu2[0], sq + nu2[1]
                    both = num * pl.reciprocal(a0 * a1, approx=True)
                    kbuf[t, side, p, bi, 0, to, :] = (both * a1).astype(BF)
                    kbuf[t, side, p, bi, 1, to, :] = (both * a0).astype(BF)
            return c

        lax.fori_loop(0, 4, chunk, 0)

    def pieces(p, part):
        if p == 0:
            return [(2 * part, quarter_of(a), lax.div(lax.rem(y + 2 * part, YS), 2)) for a in range(4)]
        below, above = lax.div(lax.rem(y + 3, YS), 2), lax.div(lax.rem(y + 1, YS), 2)
        if part == 0:
            return [(1, quarter_of(1), below), (1, quarter_of(0), below), (3, quarter_of(0), above), (3, quarter_of(2), above)]
        return [(1, quarter_of(3), below), (1, quarter_of(2), below), (3, quarter_of(1), above), (3, quarter_of(3), above)]

    def block_pieces(p, r):
        j = lax.rem(y - (r * 2 + lax.rem(y_lo + p, 2)) + YS, YS)
        return [(j, q, r) for q in range(4)]

    def product(t, p, some, bi, e):
        left = jnp.concatenate([et[j, q, bi] for j, q, r in some], axis=1)
        right = []
        for j, q, r in some:
            rows = pl.ds(pl.multiple_of(r * 512 + q * 128, 128), 128)
            right.append(jnp.concatenate([kbuf[t, side, p, bi, e, rows, :] for side in range(2)], axis=1))
        return jnp.dot(left, jnp.concatenate(right, axis=0), preferred_element_type=F32)

    def first(t, p, part, some):
        for bi in range(2):
            for e in range(2):
                value = product(t, p, some, bi, e)
                if part == 0:
                    pacc[p * 4 + t, bi, e] = value
                else:
                    pbuf[p * 4 + t, bi, e] = (pacc[p * 4 + t, bi, e] + value).astype(BF)

    def whole(p, lo, hi):
        def step(t, c):
            for bi in range(2):
                for e in range(2):
                    value = product(t, p, pieces(p, 0) + pieces(p, 1), bi, e)
                    pbuf[p * 4 + t, bi, e] = value.astype(BF)
            return c
        lax.fori_loop(lo, hi, step, 0)

    def place(k, p):
        zz = lax.rem(z - k + ZS, ZS)
        j = lax.rem(y - (lax.div(zz, 4) * 2 + lax.rem(y_lo + p, 2)) + YS, YS)
        return lax.rem(x - lax.rem(zz, 4) + XS, XS), j

    def second(ts, ps, fresh, es=(0, 1)):
        for e in es:
            left, right = [], []
            for p in ps:
                for t in ts:
                    (i1, j1), (i2, j2) = place(t, p), place((8 - t) if t else 4, p)
                    for bi in range(2):
                        left.append(pbuf[p * 4 + t, bi, e])
                        right.append(jnp.concatenate([xt[i1, j1, bi], xt[i2, j2, bi]], axis=1))
            value = lax.dot_general(
                jnp.concatenate(left, axis=1), jnp.concatenate(right, axis=1), (((1,), (1,)), ((), ())),
                preferred_element_type=F32)
            tbuf[e] = value if fresh else tbuf[e] + value

    def loop(p, part, lo, hi):
        def step(t, c):
            first(t, p, part, pieces(p, part))
            return c
        lax.fori_loop(lo, hi, step, 0)

    def z_pass(d, ns):
        for n in ns:
            for k, to in ((d, d + 1), (8 - d, 7 - d)):
                zc[k, n].wait_recv()
                if to != 4 or (n < 2) == (k == d):
                    zc[to, n].start()
        if 3 in ns:
            pc[d].start()
            pc[8 - d].start()
            if d > 1:
                token_wait(d - 2)
                token(d - 1)

    def last_tokens():
        token_wait(2)
        token(3, (0,))

    def z_end():
        for n in range(4):
            zc[4, n].wait_recv()
        pc[4].start()

    def own(*ks):
        for k in ks:
            kgen(k, core)

    def other(*ks):
        for k in ks:
            pc[k].wait_recv()
            kgen(k, 1 - core)

    def token(n, ways=(0, 1)):
        for w in ways:
            pl.semaphore_signal(tok.at[w, n], inc=1, device_id=zd(1 - 2 * w), device_id_type=MESH)

    def token_wait(n, ways=(0, 1)):
        for w in ways:
            pl.semaphore_wait(tok.at[w, n], 1)

    def x_on(j):
        xp[j].wait_recv()
        xm[j].wait_recv()
        go(*xr[j])

    def y_one():
        yp[2].wait_recv()
        go(yp[6], yp[0])
        ym[3].wait_recv()
        go(xp[3], xm[3])
        go(ym[7], ym[0])
        token(0)

    def y_two():
        yp[1].wait_recv()
        go(xp[1], xm[1])
        ym[1].wait_recv()
        go(ym[5], yp[3], ym[2])
        xt[0, 1] = et[1, quarter]
        xt[0, 3] = et[3, quarter]

    def y_three():
        yp[6].wait_recv()
        go(xp[2], xm[2])
        xt[0, 2] = et[2, quarter]

    def y_four():
        yp[0].wait_recv()
        go(yp[4])

    def y_five():
        yp[3].wait_recv()
        ym[0].wait_recv()
        ym[2].wait_recv()

    def y_six():
        for c in (yp[4], ym[5], ym[7]):
            c.wait_recv()

    def start():
        go(enc, yp[2], ym[3], xp[0], xm[0], yp[1], ym[1])
        xt[0, 0] = et[0, quarter]

    def finish():
        for j in range(4):
            for c in xr[j]:
                c.wait_recv()
        second((1, 2, 3), (0, 1), True)

    pl.semaphore_wait(barrier, len(others) + swaps.astype(jnp.int32))
    every = range(4)

    @pl.when(stays)
    def _():
        for i in range(2):
            own_loads[i].wait()
        for n in every:
            zc[1, n].start()
            zc[7, n].start()
        pc[0].start()
        start()
        enc.wait_recv()
        own(0)
        z_pass(1, every)
        x_on(0)
        own(1)
        z_pass(2, (0, 1))
        own(7)
        y_one()
        z_pass(2, (2, 3))
        other(0)
        own(2, 6)
        y_two()
        z_pass(3, (0, 1))
        other(1)
        z_pass(3, (2, 3))
        other(7)
        y_three()
        loop(0, 0, 1, 2)
        x_on(3)
        own(3, 5)
        y_four()
        loop(1, 0, 1, 2)
        other(2)
        x_on(1)
        z_end()
        last_tokens()
        other(6)
        loop(0, 0, 2, 3)
        own(4)
        loop(1, 0, 2, 3)
        y_five()
        x_on(2)
        other(3)
        loop(1, 1, 1, 3)
        other(5)
        loop(0, 0, 3, 4)
        whole(1, 3, 4)
        y_six()
        loop(0, 1, 1, 4)
        for p in range(2):
            first(0, p, 0, block_pieces(p, core))
        finish()
        other(4)
        for p in range(2):
            first(0, p, 1, block_pieces(p, 1 - core))

    @pl.when(swaps)
    def _():
        for c in swap_copies:
            c.start()
        start()
        for n in every:
            swap_copies[n].wait_recv()
            zc[1, n].start()
            zc[7, n].start()
        pc[0].start()
        enc.wait_recv()
        x_on(0)
        other(0)
        own(0)
        other(1)
        z_pass(1, (0,))
        y_one()
        z_pass(1, (1, 2, 3))
        own(1)
        y_two()
        own(7)
        other(7)
        z_pass(2, (0, 1))
        loop(0, 0, 1, 2)
        other(2)
        y_three()
        z_pass(2, (2, 3))
        loop(1, 0, 1, 2)
        other(6)
        x_on(3)
        own(2)
        z_pass(3, (0, 1))
        y_four()
        own(6)
        loop(0, 0, 2, 3)
        x_on(1)
        other(3)
        z_pass(3, (2, 3))
        own(3)
        y_five()
        x_on(2)
        last_tokens()
        other(5)
        own(5)
        loop(1, 1, 1, 2)
        loop(0, 0, 3, 4)
        whole(1, 2, 4)
        other(4)
        y_six()
        loop(0, 1, 1, 4)
        for p in range(2):
            first(0, p, 0, block_pieces(p, 1 - core))
        z_end()
        finish()
        own(4)
        for p in range(2):
            first(0, p, 1, block_pieces(p, core))

    core_copies = []
    for e in range(2):
        second((0,), (0, 1), False, (e,))
        for i in range(16):
            for c in range(2):
                acc[c, e, i] = tbuf[e, (i * 2 + c) * 8:(i * 2 + c + 1) * 8, :] * scale
        core_copies.append(copy(acc.at[1 - core, e], rc.at[e], c_s.at[e], c_r.at[e], peer))
        go(core_copies[e])
    token_wait(3, (0,))
    for e in range(2):
        core_copies[e].wait_recv()
    for i in range(16):
        both = jnp.concatenate([rc[e, i] + acc[core, e, i] for e in range(2)], axis=0)
        sb[i] = both.astype(BF)
    mine = z * 2 + y_lo
    rz_copies = []
    far_first = sorted(range(1, 16), key=lambda i: -(min(i // 2, ZS - i // 2) + i % 2))
    for i in far_first:
        k, flip = i // 2, i % 2
        to = lax.rem(z + k, ZS) * 2 + lax.rem(y_lo + flip, 2)
        rz_copies.append(copy(sb.at[to], rz.at[i], rz_s.at[i], rz_r.at[i], sum_partner(i)))
    go(*rz_copies)
    total = jnp.concatenate([rc[e, mine] + acc[core, e, mine] for e in range(2)], axis=0)
    for c in rz_copies:
        c.wait_recv()
    for i in range(1, 16):
        total = total + rz[i].astype(F32)
    for half in range(2):
        fin[half] = total[:, half * 128:(half + 1) * 128]
    rp_copies = [copy(fin.at[lax.div(lax.rem(pw + i, 8), 4)], rp.at[i], rp_s.at[i], rp_r.at[i], pw_partner(i))
                 for i in (6, 2, 5, 3, 7, 1, 4)]
    go(*rp_copies)
    for c in rp_copies:
        c.wait_recv()
    total = fin[y_hi]
    for i in range(1, 8):
        total = total + rp[i]
    for e in range(2):
        out_ref[e] = total[e * 8:(e + 1) * 8, :]
    for c in started:
        c.wait_send()
    for c in list(zc.values()) + pc:
        c.wait_send()

    @pl.when(swaps)
    def _():
        for c in swap_copies:
            c.wait_send()


def on_device(elements, strength, pole_freq, energies, imag_freqs):
    scale = 1.0 / (4096 * math.sqrt(64))
    vm = pl.BlockSpec(memory_space=pltpu.VMEM)
    hbm = pl.BlockSpec(memory_space=pltpu.HBM)
    dma = pltpu.SemaphoreType.DMA
    out = pl.pallas_call(
        lambda *refs: body(scale, *refs),
        out_shape=jax.ShapeDtypeStruct((2, 8, 128), F32),
        in_specs=[hbm] * 5,
        out_specs=vm,
        scratch_shapes=[
            pltpu.VMEM((2, 512, 256), BF),
            pltpu.SMEM((2,), F32),
            pltpu.SMEM((2,), F32),
            pltpu.VMEM((8, 2, 2, 512, 128), BF),
            pltpu.VMEM((4, 4, 2, 256, 128), BF),
            pltpu.VMEM((4, 4, 2, 256, 128), BF),
            pltpu.VMEM((2, 2, 8, 128), F32),
            pltpu.VMEM((4, 2, 2, 2, 2, 1024, 128), BF),
            pltpu.VMEM((8, 2, 2, 256, 256), F32),
            pltpu.VMEM((8, 2, 2, 256, 256), BF),
            pltpu.VMEM((2, 256, 256), F32),
            pltpu.VMEM((2, 16, 8, 256), F32),
            pltpu.VMEM((2, 2, 16, 8, 256), F32),
            pltpu.VMEM((16, 16, 256), BF),
            pltpu.VMEM((16, 16, 256), BF),
            pltpu.VMEM((2, 16, 128), F32),
            pltpu.VMEM((8, 16, 128), F32),
            dma((6,)),
            dma((4,)), dma((4,)),
            dma((8, 4)), dma((8, 4)),
            dma((8,)), dma((8,)),
            dma((3, 4)), dma((3, 4)),
            dma((4, 4)), dma((4, 4)),
            dma, dma,
            dma((2,)), dma((2,)),
            dma((16,)), dma((16,)),
            dma((8,)), dma((8,)),
            pltpu.SemaphoreType.REGULAR((2, 4)),
        ],
        compiler_params=pltpu.CompilerParams(
            collective_id=0, has_side_effects=True, vmem_limit_bytes=63 * 1024 * 1024),
        cost_estimate=pl.CostEstimate(flops=6_500_000_000, bytes_accessed=1_000_000, transcendentals=8_000_000),
        name="self_energy",
    )(elements, strength, pole_freq, energies, imag_freqs)
    return lax.dynamic_slice_in_dim(out, lax.rem(lax.axis_index("pw"), 4) * 32, 32, 2)


def solution(mesh):
    in_specs = (P("band", "pw", None), P("pw", "band"), P("pw", "band"), P("band"), P())
    out_specs = P(None, "band", "pw")
    return jax.shard_map(
        on_device, mesh=mesh, in_specs=in_specs, out_specs=out_specs, check_vma=False
    )
```

```python
import math

import jax
import jax.numpy as jnp
from jax import lax
from jax.experimental import pallas as pl
from jax.experimental.pallas import tpu as pltpu
from jax.sharding import PartitionSpec as P

MESH = pl.DeviceIdType.MESH
XS, YS, ZS = 4, 4, 8
BF = jnp.bfloat16
F32 = jnp.float32


def body(scale, e_hbm, s_hbm, w_hbm, en_hbm, nu_hbm, out_ref,
         e_vm, en_sm, nu_sm, sw, et, xt, en, kbuf, pacc, pbuf, tbuf, rc, acc, sb, rz, fin, rp,
         in_s, swap_s, swap_r, z_s, z_r, p_s, p_r, y_s, y_r, x_s, x_r, en_s, en_r,
         c_s, c_r, rz_s, rz_r, rp_s, rp_r, tok):
    band, pw = lax.axis_index("band"), lax.axis_index("pw")
    z, y_lo, core = lax.div(band, 4), lax.rem(lax.div(band, 2), 2), lax.rem(band, 2)
    y_hi, x = lax.div(pw, 4), lax.rem(pw, 4)
    y = y_hi * 2 + y_lo

    def quarter_of(k):
        yy = lax.rem(y + k + YS, YS)
        return lax.rem(yy, 2) * 2 + lax.div(yy, 2)

    quarter = quarter_of(0)

    def dev(xx, yy, zz, cc):
        return ((zz * 2 + lax.rem(yy, 2)) * 2 + cc, lax.div(yy, 2) * 4 + xx)

    def zd(k):
        return dev(x, y, lax.rem(z + k + ZS, ZS), core)

    def yd(k):
        return dev(x, lax.rem(y + k + YS, YS), z, core)

    def xd(k):
        return dev(lax.rem(x + k + XS, XS), y, z, core)

    peer = dev(x, y, z, 1 - core)
    swapper = dev(x, core * 2 + y_lo, z, y_hi)
    swaps = y_hi != core
    stays = jnp.logical_not(swaps)

    def sum_partner(i):
        k, flip = i // 2, i % 2
        return dev(x, y_hi * 2 + lax.rem(y_lo + flip, 2), lax.rem(z + k, ZS), core)

    def pw_partner(i):
        return (band, lax.rem(pw + i, 8))

    barrier = pltpu.get_barrier_semaphore()
    others = [zd(1), zd(-1), yd(1), yd(-1), xd(1), xd(-1), peer]
    for d in others:
        pl.semaphore_signal(barrier, inc=1, device_id=d, device_id_type=MESH)

    @pl.when(swaps)
    def _():
        pl.semaphore_signal(barrier, inc=1, device_id=swapper, device_id_type=MESH)

    loads = [pltpu.make_async_copy(e_hbm.at[b], e_vm.at[b], in_s.at[b]) for b in range(2)]
    loads.append(pltpu.make_async_copy(en_hbm, en_sm, in_s.at[2]))
    loads.append(pltpu.make_async_copy(nu_hbm, nu_sm, in_s.at[3]))
    own_loads = [pltpu.make_async_copy(r, sw.at[0, core, i], in_s.at[4 + i]) for i, r in enumerate((s_hbm, w_hbm))]
    for c in loads:
        c.start()

    @pl.when(stays)
    def _():
        for c in own_loads:
            c.start()

    for c in loads:
        c.wait()
    for i in range(2):
        en[0, i] = jnp.full((8, 128), en_sm[i], F32)
    nu2 = [nu_sm[e] * nu_sm[e] for e in range(2)]
    for q in range(4):
        for b in range(2):
            et[0, q, b] = e_vm[b, q * 128:(q + 1) * 128, :].T

    def copy(src, dst, ss, rs, d):
        return pltpu.make_async_remote_copy(
            src_ref=src, dst_ref=dst, send_sem=ss, recv_sem=rs, device_id=d, device_id_type=MESH)

    started = []

    def go(*copies):
        for c in copies:
            c.start()
            if all(c is not o for o in started):
                started.append(c)

    chunks = [(i, pl.ds(h * 256, 256)) for i in range(2) for h in range(2)]
    own_refs = (s_hbm, w_hbm)
    swap_copies = [copy(own_refs[i].at[rows, :], sw.at[0, y_hi, i, rows, :], swap_s.at[n], swap_r.at[n], swapper)
                   for n, (i, rows) in enumerate(chunks)]

    zc = {}
    for n, (i, rows) in enumerate(chunks):
        for k in (1, 2, 3) + ((4,) if i == 0 else ()):
            zc[k, n] = copy(sw.at[k - 1, core, i, rows, :], sw.at[k, core, i, rows, :], z_s.at[k, n], z_r.at[k, n], zd(1))
        for k in (7, 6, 5) + ((4,) if i == 1 else ()):
            zc[k, n] = copy(sw.at[(k + 1) % 8, core, i, rows, :], sw.at[k, core, i, rows, :], z_s.at[k, n], z_r.at[k, n],
                            zd(-1))
    pc = [copy(sw.at[k, core], sw.at[k, core], p_s.at[k], p_r.at[k], peer) for k in range(8)]

    yp, ym = {}, {}
    for a in range(4):
        q = quarter_of(a)
        yp[a] = copy(et.at[0, q], et.at[1, q], y_s.at[0, a], y_r.at[0, a], yd(1))
        ym[a] = copy(et.at[0, q], et.at[3, q], y_s.at[1, a], y_r.at[1, a], yd(-1))
    for a in (2, 0):
        q = quarter_of(a - 1)
        yp[4 + a] = copy(et.at[1, q], et.at[2, q], y_s.at[2, a], y_r.at[2, a], yd(1))
    for a in (3, 1):
        q = quarter_of(a + 1)
        ym[4 + a] = copy(et.at[3, q], et.at[2, q], y_s.at[2, a], y_r.at[2, a], yd(-1))
    enc = copy(en.at[0], en.at[1], en_s, en_r, yd(1))
    xp, xm, xr = {}, {}, {}
    for j in range(4):
        xp[j] = copy(et.at[j, quarter], xt.at[1, j], x_s.at[0, j], x_r.at[0, j], xd(1))
        xm[j] = copy(et.at[j, quarter], xt.at[3, j], x_s.at[1, j], x_r.at[1, j], xd(-1))
        xr[j] = (copy(xt.at[1, j, 0], xt.at[2, j, 0], x_s.at[2, j], x_r.at[2, j], xd(1)),
                 copy(xt.at[3, j, 1], xt.at[2, j, 1], x_s.at[3, j], x_r.at[3, j], xd(-1)))

    def kgen(k, r):
        t, side = (k, 0) if 0 <= k < 4 else ((8 - k) % 4, 1)

        def chunk(i, c):
            rows = pl.ds(pl.multiple_of(i * 128, 128), 128)
            s = sw[k, r, 0, rows, :].astype(F32)
            w = sw[k, r, 1, rows, :].astype(F32)
            to = pl.ds(pl.multiple_of(r * 512 + i * 128, 128), 128)
            for p in range(2):
                for bi in range(2):
                    v = w + en[p, bi, 0:1, :]
                    num = s * v
                    sq = v * v
                    a0, a1 = sq + nu2[0], sq + nu2[1]
                    both = num * pl.reciprocal(a0 * a1, approx=True)
                    kbuf[t, side, p, bi, 0, to, :] = (both * a1).astype(BF)
                    kbuf[t, side, p, bi, 1, to, :] = (both * a0).astype(BF)
            return c

        lax.fori_loop(0, 4, chunk, 0)

    def pieces(p, part):
        if p == 0:
            return [(2 * part, quarter_of(a), lax.div(lax.rem(y + 2 * part, YS), 2)) for a in range(4)]
        below, above = lax.div(lax.rem(y + 3, YS), 2), lax.div(lax.rem(y + 1, YS), 2)
        if part == 0:
            return [(1, quarter_of(1), below), (1, quarter_of(0), below), (3, quarter_of(0), above), (3, quarter_of(2), above)]
        return [(1, quarter_of(3), below), (1, quarter_of(2), below), (3, quarter_of(1), above), (3, quarter_of(3), above)]

    def block_pieces(p, r):
        j = lax.rem(y - (r * 2 + lax.rem(y_lo + p, 2)) + YS, YS)
        return [(j, q, r) for q in range(4)]

    def product(t, p, some, bi):
        left = jnp.concatenate([et[j, q, bi] for j, q, r in some], axis=1)
        right = []
        for j, q, r in some:
            rows = pl.ds(pl.multiple_of(r * 512 + q * 128, 128), 128)
            right.append(jnp.concatenate(
                [kbuf[t, side, p, bi, e, rows, :] for e in range(2) for side in range(2)], axis=1))
        value = jnp.dot(left, jnp.concatenate(right, axis=0), preferred_element_type=F32)
        return value[:, :256], value[:, 256:]

    def first(t, p, part, some):
        for bi in range(2):
            values = product(t, p, some, bi)
            for e in range(2):
                value = values[e]
                if part == 0:
                    pacc[p * 4 + t, bi, e] = value
                else:
                    pbuf[p * 4 + t, bi, e] = (pacc[p * 4 + t, bi, e] + value).astype(BF)

    def whole(p, lo, hi):
        def step(t, c):
            for bi in range(2):
                values = product(t, p, pieces(p, 0) + pieces(p, 1), bi)
                for e in range(2):
                    pbuf[p * 4 + t, bi, e] = values[e].astype(BF)
            return c
        lax.fori_loop(lo, hi, step, 0, unroll=True)

    def place(k, p):
        zz = lax.rem(z - k + ZS, ZS)
        j = lax.rem(y - (lax.div(zz, 4) * 2 + lax.rem(y_lo + p, 2)) + YS, YS)
        return lax.rem(x - lax.rem(zz, 4) + XS, XS), j

    def second(ts, ps, fresh, es=(0, 1)):
        for e in es:
            left, right = [], []
            for p in ps:
                for t in ts:
                    (i1, j1), (i2, j2) = place(t, p), place((8 - t) if t else 4, p)
                    for bi in range(2):
                        left.append(pbuf[p * 4 + t, bi, e])
                        right.append(jnp.concatenate([xt[i1, j1, bi], xt[i2, j2, bi]], axis=1))
            value = lax.dot_general(
                jnp.concatenate(left, axis=1), jnp.concatenate(right, axis=1), (((1,), (1,)), ((), ())),
                preferred_element_type=F32)
            tbuf[e] = value if fresh else tbuf[e] + value

    def loop(p, part, lo, hi):
        def step(t, c):
            first(t, p, part, pieces(p, part))
            return c
        lax.fori_loop(lo, hi, step, 0, unroll=True)

    def z_pass(d, ns):
        for n in ns:
            for k, to in ((d, d + 1), (8 - d, 7 - d)):
                zc[k, n].wait_recv()
                if to != 4 or (n < 2) == (k == d):
                    zc[to, n].start()
        if 3 in ns:
            pc[d].start()
            pc[8 - d].start()
            if d > 1:
                token_wait(d - 2)
                token(d - 1)

    def last_tokens():
        token_wait(2)
        token(3, (0,))

    def z_end():
        for n in range(4):
            zc[4, n].wait_recv()
        pc[4].start()

    def own(*ks):
        for k in ks:
            kgen(k, core)

    def other(*ks):
        for k in ks:
            pc[k].wait_recv()
            kgen(k, 1 - core)

    def token(n, ways=(0, 1)):
        for w in ways:
            pl.semaphore_signal(tok.at[w, n], inc=1, device_id=zd(1 - 2 * w), device_id_type=MESH)

    def token_wait(n, ways=(0, 1)):
        for w in ways:
            pl.semaphore_wait(tok.at[w, n], 1)

    def x_on(j):
        xp[j].wait_recv()
        xm[j].wait_recv()
        go(*xr[j])

    def y_one():
        yp[2].wait_recv()
        go(yp[6], yp[0])
        ym[3].wait_recv()
        go(xp[3], xm[3])
        go(ym[7], ym[0])
        token(0)

    def y_two():
        yp[1].wait_recv()
        go(xp[1], xm[1])
        ym[1].wait_recv()
        go(ym[5], yp[3], ym[2])
        xt[0, 1] = et[1, quarter]
        xt[0, 3] = et[3, quarter]

    def y_three():
        yp[6].wait_recv()
        go(xp[2], xm[2])
        xt[0, 2] = et[2, quarter]

    def y_four():
        yp[0].wait_recv()
        go(yp[4])

    def y_five():
        yp[3].wait_recv()
        ym[0].wait_recv()
        ym[2].wait_recv()

    def y_six():
        for c in (yp[4], ym[5], ym[7]):
            c.wait_recv()

    def start():
        go(enc, yp[2], ym[3], xp[0], xm[0], yp[1], ym[1])
        xt[0, 0] = et[0, quarter]

    def finish():
        for j in range(4):
            for c in xr[j]:
                c.wait_recv()
        second((1, 2, 3), (0, 1), True)

    pl.semaphore_wait(barrier, len(others) + swaps.astype(jnp.int32))
    every = range(4)

    @pl.when(stays)
    def _():
        for i in range(2):
            own_loads[i].wait()
        for n in every:
            zc[1, n].start()
            zc[7, n].start()
        pc[0].start()
        start()
        enc.wait_recv()
        own(0)
        z_pass(1, every)
        x_on(0)
        own(1)
        z_pass(2, (0, 1))
        own(7)
        y_one()
        z_pass(2, (2, 3))
        other(0)
        own(2, 6)
        y_two()
        z_pass(3, (0, 1))
        other(1)
        z_pass(3, (2, 3))
        other(7)
        y_three()
        loop(0, 0, 1, 2)
        x_on(3)
        own(3, 5)
        y_four()
        loop(1, 0, 1, 2)
        other(2)
        x_on(1)
        z_end()
        last_tokens()
        other(6)
        loop(0, 0, 2, 3)
        own(4)
        loop(1, 0, 2, 3)
        y_five()
        x_on(2)
        other(3)
        loop(1, 1, 1, 3)
        other(5)
        loop(0, 0, 3, 4)
        whole(1, 3, 4)
        y_six()
        loop(0, 1, 1, 4)
        for p in range(2):
            first(0, p, 0, block_pieces(p, core))
        finish()
        other(4)
        for p in range(2):
            first(0, p, 1, block_pieces(p, 1 - core))

    @pl.when(swaps)
    def _():
        for c in swap_copies:
            c.start()
        start()
        for n in every:
            swap_copies[n].wait_recv()
            zc[1, n].start()
            zc[7, n].start()
        pc[0].start()
        enc.wait_recv()
        x_on(0)
        other(0)
        own(0)
        other(1)
        z_pass(1, (0,))
        y_one()
        z_pass(1, (1, 2, 3))
        own(1)
        y_two()
        own(7)
        other(7)
        z_pass(2, (0, 1))
        loop(0, 0, 1, 2)
        other(2)
        y_three()
        z_pass(2, (2, 3))
        loop(1, 0, 1, 2)
        other(6)
        x_on(3)
        own(2)
        z_pass(3, (0, 1))
        y_four()
        own(6)
        loop(0, 0, 2, 3)
        x_on(1)
        other(3)
        z_pass(3, (2, 3))
        own(3)
        y_five()
        x_on(2)
        last_tokens()
        other(5)
        own(5)
        loop(1, 1, 1, 2)
        loop(0, 0, 3, 4)
        whole(1, 2, 4)
        other(4)
        y_six()
        loop(0, 1, 1, 4)
        for p in range(2):
            first(0, p, 0, block_pieces(p, 1 - core))
        z_end()
        finish()
        own(4)
        for p in range(2):
            first(0, p, 1, block_pieces(p, core))

    core_copies = []
    for e in range(2):
        second((0,), (0, 1), False, (e,))
        for i in range(16):
            for c in range(2):
                acc[c, e, i] = tbuf[e, (i * 2 + c) * 8:(i * 2 + c + 1) * 8, :] * scale
        core_copies.append(copy(acc.at[1 - core, e], rc.at[e], c_s.at[e], c_r.at[e], peer))
        go(core_copies[e])
    token_wait(3, (0,))
    for e in range(2):
        core_copies[e].wait_recv()
    for i in range(16):
        both = jnp.concatenate([rc[e, i] + acc[core, e, i] for e in range(2)], axis=0)
        sb[i] = both.astype(BF)
    mine = z * 2 + y_lo
    rz_copies = []
    far_first = sorted(range(1, 16), key=lambda i: -(min(i // 2, ZS - i // 2) + i % 2))
    for i in far_first:
        k, flip = i // 2, i % 2
        to = lax.rem(z + k, ZS) * 2 + lax.rem(y_lo + flip, 2)
        rz_copies.append(copy(sb.at[to], rz.at[i], rz_s.at[i], rz_r.at[i], sum_partner(i)))
    sent = list(started)
    go(*rz_copies)
    for c in sent + list(zc.values()) + pc:
        c.wait_send()

    @pl.when(swaps)
    def _():
        for c in swap_copies:
            c.wait_send()

    total = jnp.concatenate([rc[e, mine] + acc[core, e, mine] for e in range(2)], axis=0)
    for c in rz_copies:
        c.wait_recv()
    for i in range(1, 16):
        total = total + rz[i].astype(F32)
    for half in range(2):
        fin[half] = total[:, half * 128:(half + 1) * 128]
    rp_copies = [copy(fin.at[lax.div(lax.rem(pw + i, 8), 4)], rp.at[i], rp_s.at[i], rp_r.at[i], pw_partner(i))
                 for i in (6, 2, 5, 3, 7, 1, 4)]
    go(*rp_copies)
    for c in rz_copies:
        c.wait_send()
    for c in rp_copies:
        c.wait_recv()
    total = fin[y_hi]
    for i in range(1, 8):
        total = total + rp[i]
    for e in range(2):
        out_ref[e] = total[e * 8:(e + 1) * 8, :]
    for c in rp_copies:
        c.wait_send()


def on_device(elements, strength, pole_freq, energies, imag_freqs):
    scale = 1.0 / (4096 * math.sqrt(64))
    vm = pl.BlockSpec(memory_space=pltpu.VMEM)
    hbm = pl.BlockSpec(memory_space=pltpu.HBM)
    dma = pltpu.SemaphoreType.DMA
    out = pl.pallas_call(
        lambda *refs: body(scale, *refs),
        out_shape=jax.ShapeDtypeStruct((2, 8, 128), F32),
        in_specs=[hbm] * 5,
        out_specs=vm,
        scratch_shapes=[
            pltpu.VMEM((2, 512, 256), BF),
            pltpu.SMEM((2,), F32),
            pltpu.SMEM((2,), F32),
            pltpu.VMEM((8, 2, 2, 512, 128), BF),
            pltpu.VMEM((4, 4, 2, 256, 128), BF),
            pltpu.VMEM((4, 4, 2, 256, 128), BF),
            pltpu.VMEM((2, 2, 8, 128), F32),
            pltpu.VMEM((4, 2, 2, 2, 2, 1024, 128), BF),
            pltpu.VMEM((8, 2, 2, 256, 256), F32),
            pltpu.VMEM((8, 2, 2, 256, 256), BF),
            pltpu.VMEM((2, 256, 256), F32),
            pltpu.VMEM((2, 16, 8, 256), F32),
            pltpu.VMEM((2, 2, 16, 8, 256), F32),
            pltpu.VMEM((16, 16, 256), BF),
            pltpu.VMEM((16, 16, 256), BF),
            pltpu.VMEM((2, 16, 128), F32),
            pltpu.VMEM((8, 16, 128), F32),
            dma((6,)),
            dma((4,)), dma((4,)),
            dma((8, 4)), dma((8, 4)),
            dma((8,)), dma((8,)),
            dma((3, 4)), dma((3, 4)),
            dma((4, 4)), dma((4, 4)),
            dma, dma,
            dma((2,)), dma((2,)),
            dma((16,)), dma((16,)),
            dma((8,)), dma((8,)),
            pltpu.SemaphoreType.REGULAR((2, 4)),
        ],
        compiler_params=pltpu.CompilerParams(
            collective_id=0, has_side_effects=True, vmem_limit_bytes=63 * 1024 * 1024),
        cost_estimate=pl.CostEstimate(flops=6_500_000_000, bytes_accessed=1_000_000, transcendentals=8_000_000),
        name="self_energy",
    )(elements, strength, pole_freq, energies, imag_freqs)
    return lax.dynamic_slice_in_dim(out, lax.rem(lax.axis_index("pw"), 4) * 32, 32, 2)


def solution(mesh):
    in_specs = (P("band", "pw", None), P("pw", "band"), P("pw", "band"), P("band"), P())
    out_specs = P(None, "band", "pw")
    return jax.shard_map(
        on_device, mesh=mesh, in_specs=in_specs, out_specs=out_specs, check_vma=False
    )
```

```python
import math

import jax
import jax.numpy as jnp
from jax import lax
from jax.experimental import pallas as pl
from jax.experimental.pallas import tpu as pltpu
from jax.sharding import PartitionSpec as P

MESH = pl.DeviceIdType.MESH
XS, YS, ZS = 4, 4, 8
BF = jnp.bfloat16
F32 = jnp.float32


def body(scale, e_hbm, s_hbm, w_hbm, en_hbm, nu_hbm, out_ref,
         e_vm, en_sm, nu_sm, sw, et, xt, en, kbuf, pacc, pbuf, tbuf, rc, acc, sb, rz, fin, rp,
         in_s, swap_s, swap_r, z_s, z_r, p_s, p_r, y_s, y_r, x_s, x_r, en_s, en_r,
         c_s, c_r, rz_s, rz_r, rp_s, rp_r, tok):
    band, pw = lax.axis_index("band"), lax.axis_index("pw")
    z, y_lo, core = lax.div(band, 4), lax.rem(lax.div(band, 2), 2), lax.rem(band, 2)
    y_hi, x = lax.div(pw, 4), lax.rem(pw, 4)
    y = y_hi * 2 + y_lo

    def quarter_of(k):
        yy = lax.rem(y + k + YS, YS)
        return lax.rem(yy, 2) * 2 + lax.div(yy, 2)

    quarter = quarter_of(0)

    def dev(xx, yy, zz, cc):
        return ((zz * 2 + lax.rem(yy, 2)) * 2 + cc, lax.div(yy, 2) * 4 + xx)

    def zd(k):
        return dev(x, y, lax.rem(z + k + ZS, ZS), core)

    def yd(k):
        return dev(x, lax.rem(y + k + YS, YS), z, core)

    def xd(k):
        return dev(lax.rem(x + k + XS, XS), y, z, core)

    peer = dev(x, y, z, 1 - core)
    swapper = dev(x, core * 2 + y_lo, z, y_hi)
    swaps = y_hi != core
    stays = jnp.logical_not(swaps)

    def sum_partner(i):
        k, flip = i // 2, i % 2
        return dev(x, y_hi * 2 + lax.rem(y_lo + flip, 2), lax.rem(z + k, ZS), core)

    def pw_partner(i):
        return (band, lax.rem(pw + i, 8))

    barrier = pltpu.get_barrier_semaphore()
    others = [zd(1), zd(-1), yd(1), yd(-1), xd(1), xd(-1), peer]
    for d in others:
        pl.semaphore_signal(barrier, inc=1, device_id=d, device_id_type=MESH)

    @pl.when(swaps)
    def _():
        pl.semaphore_signal(barrier, inc=1, device_id=swapper, device_id_type=MESH)

    loads = [pltpu.make_async_copy(e_hbm.at[b], e_vm.at[b], in_s.at[b]) for b in range(2)]
    loads.append(pltpu.make_async_copy(en_hbm, en_sm, in_s.at[2]))
    loads.append(pltpu.make_async_copy(nu_hbm, nu_sm, in_s.at[3]))
    own_loads = [pltpu.make_async_copy(r, sw.at[0, core, i], in_s.at[4 + i]) for i, r in enumerate((s_hbm, w_hbm))]
    for c in loads:
        c.start()

    @pl.when(stays)
    def _():
        for c in own_loads:
            c.start()

    for c in loads:
        c.wait()
    for i in range(2):
        en[0, i] = jnp.full((8, 128), en_sm[i], F32)
    nu2 = [nu_sm[e] * nu_sm[e] for e in range(2)]
    for q in range(4):
        for b in range(2):
            et[0, q, b] = e_vm[b, q * 128:(q + 1) * 128, :].T

    def copy(src, dst, ss, rs, d):
        return pltpu.make_async_remote_copy(
            src_ref=src, dst_ref=dst, send_sem=ss, recv_sem=rs, device_id=d, device_id_type=MESH)

    started = []

    def go(*copies):
        for c in copies:
            c.start()
            if all(c is not o for o in started):
                started.append(c)

    chunks = [(i, pl.ds(h * 256, 256)) for i in range(2) for h in range(2)]
    own_refs = (s_hbm, w_hbm)
    swap_copies = [copy(own_refs[i].at[rows, :], sw.at[0, y_hi, i, rows, :], swap_s.at[n], swap_r.at[n], swapper)
                   for n, (i, rows) in enumerate(chunks)]

    zc = {}
    for n, (i, rows) in enumerate(chunks):
        for k in (1, 2, 3) + ((4,) if i == 0 else ()):
            zc[k, n] = copy(sw.at[k - 1, core, i, rows, :], sw.at[k, core, i, rows, :], z_s.at[k, n], z_r.at[k, n], zd(1))
        for k in (7, 6, 5) + ((4,) if i == 1 else ()):
            zc[k, n] = copy(sw.at[(k + 1) % 8, core, i, rows, :], sw.at[k, core, i, rows, :], z_s.at[k, n], z_r.at[k, n],
                            zd(-1))
    pc = [copy(sw.at[k, core], sw.at[k, core], p_s.at[k], p_r.at[k], peer) for k in range(8)]

    yp, ym = {}, {}
    for a in range(4):
        q = quarter_of(a)
        yp[a] = copy(et.at[0, q], et.at[1, q], y_s.at[0, a], y_r.at[0, a], yd(1))
        ym[a] = copy(et.at[0, q], et.at[3, q], y_s.at[1, a], y_r.at[1, a], yd(-1))
    for a in (2, 0):
        q = quarter_of(a - 1)
        yp[4 + a] = copy(et.at[1, q], et.at[2, q], y_s.at[2, a], y_r.at[2, a], yd(1))
    for a in (3, 1):
        q = quarter_of(a + 1)
        ym[4 + a] = copy(et.at[3, q], et.at[2, q], y_s.at[2, a], y_r.at[2, a], yd(-1))
    enc = copy(en.at[0], en.at[1], en_s, en_r, yd(1))
    xp, xm, xr = {}, {}, {}
    for j in range(4):
        xp[j] = copy(et.at[j, quarter], xt.at[1, j], x_s.at[0, j], x_r.at[0, j], xd(1))
        xm[j] = copy(et.at[j, quarter], xt.at[3, j], x_s.at[1, j], x_r.at[1, j], xd(-1))
        xr[j] = (copy(xt.at[1, j, 0], xt.at[2, j, 0], x_s.at[2, j], x_r.at[2, j], xd(1)),
                 copy(xt.at[3, j, 1], xt.at[2, j, 1], x_s.at[3, j], x_r.at[3, j], xd(-1)))

    def kgen(k, r):
        t, side = (k, 0) if 0 <= k < 4 else ((8 - k) % 4, 1)

        def chunk(i, c):
            rows = pl.ds(pl.multiple_of(i * 128, 128), 128)
            s = sw[k, r, 0, rows, :].astype(F32)
            w = sw[k, r, 1, rows, :].astype(F32)
            to = pl.ds(pl.multiple_of(r * 512 + i * 128, 128), 128)
            for p in range(2):
                for bi in range(2):
                    v = w + en[p, bi, 0:1, :]
                    num = s * v
                    sq = v * v
                    a0, a1 = sq + nu2[0], sq + nu2[1]
                    both = num * pl.reciprocal(a0 * a1, approx=True)
                    kbuf[t, side, p, bi, 0, to, :] = (both * a1).astype(BF)
                    kbuf[t, side, p, bi, 1, to, :] = (both * a0).astype(BF)
            return c

        lax.fori_loop(0, 4, chunk, 0)

    def pieces(p, part):
        if p == 0:
            return [(2 * part, quarter_of(a), lax.div(lax.rem(y + 2 * part, YS), 2)) for a in range(4)]
        below, above = lax.div(lax.rem(y + 3, YS), 2), lax.div(lax.rem(y + 1, YS), 2)
        if part == 0:
            return [(1, quarter_of(1), below), (1, quarter_of(0), below), (3, quarter_of(0), above), (3, quarter_of(2), above)]
        return [(1, quarter_of(3), below), (1, quarter_of(2), below), (3, quarter_of(1), above), (3, quarter_of(3), above)]

    def block_pieces(p, r):
        j = lax.rem(y - (r * 2 + lax.rem(y_lo + p, 2)) + YS, YS)
        return [(j, q, r) for q in range(4)]

    def product(t, p, some, bi):
        left = jnp.concatenate([et[j, q, bi] for j, q, r in some], axis=1)
        right = []
        for j, q, r in some:
            rows = pl.ds(pl.multiple_of(r * 512 + q * 128, 128), 128)
            right.append(jnp.concatenate(
                [kbuf[t, side, p, bi, e, rows, :] for e in range(2) for side in range(2)], axis=1))
        value = jnp.dot(left, jnp.concatenate(right, axis=0), preferred_element_type=F32)
        return value[:, :256], value[:, 256:]

    def first(t, p, part, some):
        for bi in range(2):
            values = product(t, p, some, bi)
            for e in range(2):
                value = values[e]
                if part == 0:
                    pacc[p * 4 + t, bi, e] = value
                else:
                    pbuf[p * 4 + t, bi, e] = (pacc[p * 4 + t, bi, e] + value).astype(BF)

    def whole(p, lo, hi):
        def step(t, c):
            for bi in range(2):
                values = product(t, p, pieces(p, 0) + pieces(p, 1), bi)
                for e in range(2):
                    pbuf[p * 4 + t, bi, e] = values[e].astype(BF)
            return c
        lax.fori_loop(lo, hi, step, 0, unroll=True)

    def place(k, p):
        zz = lax.rem(z - k + ZS, ZS)
        j = lax.rem(y - (lax.div(zz, 4) * 2 + lax.rem(y_lo + p, 2)) + YS, YS)
        return lax.rem(x - lax.rem(zz, 4) + XS, XS), j

    def second(ts, ps, fresh, es=(0, 1)):
        for e in es:
            left, right = [], []
            for p in ps:
                for t in ts:
                    (i1, j1), (i2, j2) = place(t, p), place((8 - t) if t else 4, p)
                    for bi in range(2):
                        left.append(pbuf[p * 4 + t, bi, e])
                        right.append(jnp.concatenate([xt[i1, j1, bi], xt[i2, j2, bi]], axis=1))
            value = lax.dot_general(
                jnp.concatenate(left, axis=1), jnp.concatenate(right, axis=1), (((1,), (1,)), ((), ())),
                preferred_element_type=F32)
            tbuf[e] = value if fresh else tbuf[e] + value

    def loop(p, part, lo, hi):
        def step(t, c):
            first(t, p, part, pieces(p, part))
            return c
        lax.fori_loop(lo, hi, step, 0, unroll=True)

    def z_pass(d, ns):
        for n in ns:
            for k, to in ((d, d + 1), (8 - d, 7 - d)):
                zc[k, n].wait_recv()
                if to != 4 or (n < 2) == (k == d):
                    zc[to, n].start()
        if 3 in ns:
            pc[d].start()
            pc[8 - d].start()
            if d > 1:
                token_wait(d - 2)
                token(d - 1)

    def last_tokens():
        token_wait(2)
        token(3, (0,))

    def z_end():
        for n in range(4):
            zc[4, n].wait_recv()
        pc[4].start()

    def own(*ks):
        for k in ks:
            kgen(k, core)

    def other(*ks):
        for k in ks:
            pc[k].wait_recv()
            kgen(k, 1 - core)

    def token(n, ways=(0, 1)):
        for w in ways:
            pl.semaphore_signal(tok.at[w, n], inc=1, device_id=zd(1 - 2 * w), device_id_type=MESH)

    def token_wait(n, ways=(0, 1)):
        for w in ways:
            pl.semaphore_wait(tok.at[w, n], 1)

    def x_on(j):
        xp[j].wait_recv()
        xm[j].wait_recv()
        go(*xr[j])

    def y_one():
        yp[2].wait_recv()
        go(yp[6], yp[0])
        ym[3].wait_recv()
        go(xp[3], xm[3])
        go(ym[7], ym[0])
        token(0)

    def y_two():
        yp[1].wait_recv()
        go(xp[1], xm[1])
        ym[1].wait_recv()
        go(ym[5], yp[3], ym[2])
        xt[0, 1] = et[1, quarter]
        xt[0, 3] = et[3, quarter]

    def y_three():
        yp[6].wait_recv()
        go(xp[2], xm[2])
        xt[0, 2] = et[2, quarter]

    def y_four():
        yp[0].wait_recv()
        go(yp[4])

    def y_five():
        yp[3].wait_recv()
        ym[0].wait_recv()
        ym[2].wait_recv()

    def y_six():
        for c in (yp[4], ym[5], ym[7]):
            c.wait_recv()

    def start():
        go(enc, yp[2], ym[3], xp[0], xm[0], yp[1], ym[1])
        xt[0, 0] = et[0, quarter]

    def finish():
        for j in range(4):
            for c in xr[j]:
                c.wait_recv()
        second((1, 2, 3), (0, 1), True)

    pl.semaphore_wait(barrier, len(others) + swaps.astype(jnp.int32))
    every = range(4)

    @pl.when(stays)
    def _():
        for i in range(2):
            own_loads[i].wait()
        for n in every:
            zc[1, n].start()
            zc[7, n].start()
        pc[0].start()
        start()
        enc.wait_recv()
        own(0)
        z_pass(1, every)
        x_on(0)
        own(1)
        z_pass(2, (0, 1))
        own(7)
        y_one()
        z_pass(2, (2, 3))
        other(0)
        own(2, 6)
        y_two()
        z_pass(3, (0, 1))
        other(1)
        z_pass(3, (2, 3))
        other(7)
        y_three()
        loop(0, 0, 1, 2)
        x_on(3)
        own(3, 5)
        y_four()
        loop(1, 0, 1, 2)
        other(2)
        x_on(1)
        z_end()
        last_tokens()
        other(6)
        loop(0, 0, 2, 3)
        own(4)
        loop(1, 0, 2, 3)
        y_five()
        x_on(2)
        other(3)
        loop(1, 1, 1, 3)
        other(5)
        loop(0, 0, 3, 4)
        whole(1, 3, 4)
        y_six()
        loop(0, 1, 1, 4)
        for p in range(2):
            first(0, p, 0, block_pieces(p, core))
        finish()
        other(4)
        for p in range(2):
            first(0, p, 1, block_pieces(p, 1 - core))

    @pl.when(swaps)
    def _():
        for c in swap_copies:
            c.start()
        start()
        for n in every:
            swap_copies[n].wait_recv()
            zc[1, n].start()
            zc[7, n].start()
        pc[0].start()
        enc.wait_recv()
        x_on(0)
        other(0)
        own(0)
        other(1)
        z_pass(1, (0,))
        y_one()
        z_pass(1, (1, 2, 3))
        own(1)
        y_two()
        own(7)
        other(7)
        z_pass(2, (0, 1))
        loop(0, 0, 1, 2)
        other(2)
        y_three()
        z_pass(2, (2, 3))
        loop(1, 0, 1, 2)
        other(6)
        x_on(3)
        own(2)
        z_pass(3, (0, 1))
        y_four()
        own(6)
        loop(0, 0, 2, 3)
        x_on(1)
        other(3)
        z_pass(3, (2, 3))
        own(3)
        y_five()
        x_on(2)
        last_tokens()
        other(5)
        own(5)
        loop(1, 1, 1, 2)
        loop(0, 0, 3, 4)
        whole(1, 2, 4)
        other(4)
        y_six()
        loop(0, 1, 1, 4)
        z_end()
        for p in range(2):
            first(0, p, 0, block_pieces(p, 1 - core))
        finish()
        own(4)
        for p in range(2):
            first(0, p, 1, block_pieces(p, core))

    core_copies = []
    for e in range(2):
        second((0,), (0, 1), False, (e,))
        for i in range(16):
            for c in range(2):
                acc[c, e, i] = tbuf[e, (i * 2 + c) * 8:(i * 2 + c + 1) * 8, :] * scale
        core_copies.append(copy(acc.at[1 - core, e], rc.at[e], c_s.at[e], c_r.at[e], peer))
        go(core_copies[e])
    token_wait(3, (0,))
    for e in range(2):
        core_copies[e].wait_recv()
    for i in range(16):
        both = jnp.concatenate([rc[e, i] + acc[core, e, i] for e in range(2)], axis=0)
        sb[i] = both.astype(BF)
    mine = z * 2 + y_lo
    rz_copies = []
    far_first = sorted(range(1, 16), key=lambda i: -(min(i // 2, ZS - i // 2) + i % 2))
    for i in far_first:
        k, flip = i // 2, i % 2
        to = lax.rem(z + k, ZS) * 2 + lax.rem(y_lo + flip, 2)
        rz_copies.append(copy(sb.at[to], rz.at[i], rz_s.at[i], rz_r.at[i], sum_partner(i)))
    sent = list(started)
    go(*rz_copies)
    for c in sent + list(zc.values()) + pc:
        c.wait_send()

    @pl.when(swaps)
    def _():
        for c in swap_copies:
            c.wait_send()

    total = jnp.concatenate([rc[e, mine] + acc[core, e, mine] for e in range(2)], axis=0)
    for c in rz_copies:
        c.wait_recv()
    for i in range(1, 16):
        total = total + rz[i].astype(F32)
    for half in range(2):
        fin[half] = total[:, half * 128:(half + 1) * 128]
    rp_copies = [copy(fin.at[lax.div(lax.rem(pw + i, 8), 4)], rp.at[i], rp_s.at[i], rp_r.at[i], pw_partner(i))
                 for i in (6, 2, 5, 3, 7, 1, 4)]
    go(*rp_copies)
    for c in rz_copies:
        c.wait_send()
    for c in rp_copies:
        c.wait_recv()
    total = fin[y_hi]
    for i in range(1, 8):
        total = total + rp[i]
    for e in range(2):
        out_ref[e] = total[e * 8:(e + 1) * 8, :]
    for c in rp_copies:
        c.wait_send()


def on_device(elements, strength, pole_freq, energies, imag_freqs):
    scale = 1.0 / (4096 * math.sqrt(64))
    vm = pl.BlockSpec(memory_space=pltpu.VMEM)
    hbm = pl.BlockSpec(memory_space=pltpu.HBM)
    dma = pltpu.SemaphoreType.DMA
    out = pl.pallas_call(
        lambda *refs: body(scale, *refs),
        out_shape=jax.ShapeDtypeStruct((2, 8, 128), F32),
        in_specs=[hbm] * 5,
        out_specs=vm,
        scratch_shapes=[
            pltpu.VMEM((2, 512, 256), BF),
            pltpu.SMEM((2,), F32),
            pltpu.SMEM((2,), F32),
            pltpu.VMEM((8, 2, 2, 512, 128), BF),
            pltpu.VMEM((4, 4, 2, 256, 128), BF),
            pltpu.VMEM((4, 4, 2, 256, 128), BF),
            pltpu.VMEM((2, 2, 8, 128), F32),
            pltpu.VMEM((4, 2, 2, 2, 2, 1024, 128), BF),
            pltpu.VMEM((8, 2, 2, 256, 256), F32),
            pltpu.VMEM((8, 2, 2, 256, 256), BF),
            pltpu.VMEM((2, 256, 256), F32),
            pltpu.VMEM((2, 16, 8, 256), F32),
            pltpu.VMEM((2, 2, 16, 8, 256), F32),
            pltpu.VMEM((16, 16, 256), BF),
            pltpu.VMEM((16, 16, 256), BF),
            pltpu.VMEM((2, 16, 128), F32),
            pltpu.VMEM((8, 16, 128), F32),
            dma((6,)),
            dma((4,)), dma((4,)),
            dma((8, 4)), dma((8, 4)),
            dma((8,)), dma((8,)),
            dma((3, 4)), dma((3, 4)),
            dma((4, 4)), dma((4, 4)),
            dma, dma,
            dma((2,)), dma((2,)),
            dma((16,)), dma((16,)),
            dma((8,)), dma((8,)),
            pltpu.SemaphoreType.REGULAR((2, 4)),
        ],
        compiler_params=pltpu.CompilerParams(
            collective_id=0, has_side_effects=True, vmem_limit_bytes=63 * 1024 * 1024),
        cost_estimate=pl.CostEstimate(flops=6_500_000_000, bytes_accessed=1_000_000, transcendentals=8_000_000),
        name="self_energy",
    )(elements, strength, pole_freq, energies, imag_freqs)
    return lax.dynamic_slice_in_dim(out, lax.rem(lax.axis_index("pw"), 4) * 32, 32, 2)


def solution(mesh):
    in_specs = (P("band", "pw", None), P("pw", "band"), P("pw", "band"), P("band"), P())
    out_specs = P(None, "band", "pw")
    return jax.shard_map(
        on_device, mesh=mesh, in_specs=in_specs, out_specs=out_specs, check_vma=False
    )
```
